128 devices in a mesh: frame: 16 (over x_lo, y, core), head: 8 (over z, x_hi).
Axes of the slice: x: 4 (x_hi: 2, x_lo: 2; x = x_hi * 2 + x_lo), y: 4, z: 4, core: 2. Of those that a mesh axis runs over, the one named last changes fastest.
Arguments:
- queries: bfloat16 [12288, 40, 128], P('frame', 'head')
- keys_values: bfloat16 [2, 12288, 40, 128], P(None, 'frame', 'head')
- head_kind: int32 [40], P('head'), may hold values from 0 to 1, as said below
- tile_neighbours: int32 [32, 2], P('frame'), may hold values from 0 to 31, as said below
- tile_mask: int32 [32, 2], P('frame'), may hold values 0 or 1
- out_weight: bfloat16 [5120, 5120], P('head'), may hold values from -0.078125 to 0.078125
Outputs:
- projected: bfloat16 [12288, 5120], P(('frame', 'head'))
The draws below stay inside these ranges and needn't reach their ends.
Inputs may be any that keep to these rules, and one draw needn't show every extreme that they name: `head_kind`: each aligned block of 5 heads holds at most 2 temporal heads, and some block holds exactly 2. `tile_neighbours`: row g names 2 distinct tiles other than g, each in the partition of g (partition g // 2), among the last 1 tiles of the partition before it, or among the first 1 tiles of the partition after it.
All inputs are finite; a program needn't handle non-finite values. No bound on the sum of `tile_mask` on one device may be relied on, other than what follows from the above.
Results may differ from the reference program's by a relative error of at most 0.015.
Values may be sent and summed in bfloat16 or wider, within the bound.
A program may use at most 128 MiB of HBM per device.

```python
import jax
import jax.numpy as jnp
from jax import lax

D = 5120
HEADS = 40
HD = 128
TILE = 384
NBR = 2
FACE = 1
TILES_DEV = 2
TOK_DEV = 768
TILES = 32
TOKENS = 12288
HEADS_DEV = 5
TMAX = 2


def attention_rows(key):
    base_key = jax.random.fold_in(key, 11)
    query_draw = jax.random.normal(jax.random.fold_in(base_key, 1), (TOKENS, HEADS, HD), jnp.float32)
    key_draw = jax.random.normal(jax.random.fold_in(base_key, 2), (TOKENS, HEADS, HD), jnp.float32)
    value_draw = jax.random.normal(jax.random.fold_in(base_key, 5), (TOKENS, HEADS, HD), jnp.float32)
    return (query_draw, jnp.stack([key_draw, value_draw], axis=0))


def draw_queries(key, part):
    return attention_rows(key)[0].astype(jnp.bfloat16)


def draw_keys_values(key, part):
    return attention_rows(key)[1].astype(jnp.bfloat16)


def draw_head_kind(key, part):
    block_count = HEADS // HEADS_DEV
    counts = jax.random.randint(jax.random.fold_in(key, 21), (block_count,), 0, TMAX + 1)
    forced = jax.random.randint(jax.random.fold_in(key, 22), (), 0, block_count)
    counts = jnp.where(jnp.arange(block_count) == forced, TMAX, counts)
    block_keys = jax.random.split(jax.random.fold_in(key, 23), block_count)
    orders = jax.vmap(lambda block_key: jax.random.permutation(block_key, HEADS_DEV))(block_keys)
    return (orders < counts[:, None]).astype(jnp.int32).reshape(HEADS)


def draw_tile_neighbours(key, part):
    window = TILES_DEV + 2 * FACE
    tile_ids = jnp.arange(TILES, dtype=jnp.int32)
    partition = tile_ids // TILES_DEV
    within = tile_ids % TILES_DEV
    candidates = jnp.arange(window, dtype=jnp.int32)
    global_ids = partition[:, None] * TILES_DEV - FACE + candidates[None, :]
    usable = (global_ids >= 0) & (global_ids < TILES) & (candidates[None, :] != FACE + within[:, None])
    tile_keys = jax.random.split(jax.random.fold_in(key, 31), TILES)
    ranks = jax.vmap(lambda tile_key: jax.random.permutation(tile_key, window))(tile_keys).astype(jnp.int32)
    ranks = jnp.where(usable, ranks, -1)
    unused, picked = lax.top_k(ranks, NBR)
    return jnp.take_along_axis(global_ids, picked, axis=1).astype(jnp.int32)


def with_ends(values, key, least, largest):
    longest = values.shape.index(max(values.shape))
    spots = []
    for shift in (0, 1):
        where = [jax.random.randint(jax.random.fold_in(key, axis), (), 0, length) for axis, length in enumerate(values.shape)]
        where[longest] = (where[longest] + shift) % values.shape[longest]
        spots.append(tuple(where))
    return values.at[spots[0]].set(least).at[spots[1]].set(largest)


def block_levels(own_key, dims, cuts, low, largest):
    level = 1.0
    for dim, shards_of in cuts:
        heights = jax.random.uniform(jax.random.fold_in(jax.random.fold_in(own_key, 6), dim), (shards_of,), jnp.float32, low / len(cuts), largest / len(cuts))
        level = level * jnp.repeat(jnp.exp(heights), dims[dim] // shards_of).reshape((-1,) + (1,) * (len(dims) - 1 - dim))
    return level


def scatter_about(key, extent, scale, most, cuts=(), kind=jnp.bfloat16):
    entries = jax.random.normal(key, extent, jnp.float32) * scale
    if len(cuts) > 0:
        entries = block_levels(key, extent, cuts, -0.22, 0.18) * entries
    return jnp.clip(entries, min=-most, max=most).astype(kind)


def setup_inputs(seed: int = 0) -> dict:
    key_list = jax.random.split(jax.random.key(seed), 7)
    return {
        "queries": draw_queries(jax.random.fold_in(key_list[6], 71), 0),
        "keys_values": draw_keys_values(jax.random.fold_in(key_list[6], 71), 0),
        "head_kind": draw_head_kind(jax.random.fold_in(key_list[6], 71), 0),
        "tile_neighbours": draw_tile_neighbours(jax.random.fold_in(key_list[6], 71), 0),
        "tile_mask": with_ends((jax.random.randint(key_list[4], (TILES, NBR), 0, 3) < 2).astype(jnp.int32), jax.random.fold_in(key_list[4], 1), 0, 1),
        "out_weight": scatter_about(key_list[5], (HEADS * HD, D), (HEADS * HD) ** -0.5, 0.078125, ((0, 8),)),
    }


def reference(queries, keys_values, head_kind, tile_neighbours, tile_mask, out_weight):
    score_scale = HD ** -0.5
    query_heads = jnp.transpose(queries, (1, 0, 2))
    key_heads = jnp.transpose(keys_values[0], (1, 0, 2))
    value_heads = jnp.transpose(keys_values[1], (1, 0, 2))
    own_tiles = jnp.arange(TILES, dtype=jnp.int32)
    key_tiles = jnp.concatenate([own_tiles[:, None], tile_neighbours.astype(jnp.int32)], axis=1)
    allowed_tiles = jnp.concatenate([jnp.ones((TILES, 1), dtype=bool), tile_mask == 1], axis=1)
    allowed_keys = jnp.repeat(allowed_tiles, TILE, axis=1)

    def global_head(query_rows, key_rows, value_rows):
        blocks = query_rows.reshape(TOKENS // TOK_DEV, TOK_DEV, HD)

        def one_block(block_rows):
            scores = jnp.dot(block_rows, key_rows.T, preferred_element_type=jnp.float32) * score_scale
            top_score = jnp.max(scores, axis=1, keepdims=True)
            exponent = jnp.exp(scores - top_score)
            weight_sum = jnp.sum(exponent, axis=1, keepdims=True)
            mixed = jnp.dot(exponent.astype(jnp.bfloat16), value_rows, preferred_element_type=jnp.float32)
            return mixed / weight_sum

        return lax.map(one_block, blocks).reshape(TOKENS, HD)

    def tile_head(query_rows, key_rows, value_rows):
        query_tiles = query_rows.reshape(TILES, TILE, HD).astype(jnp.float32)
        key_sets = key_rows.reshape(TILES, TILE, HD)[key_tiles].reshape(TILES, (NBR + 1) * TILE, HD)
        value_sets = value_rows.reshape(TILES, TILE, HD)[key_tiles].reshape(TILES, (NBR + 1) * TILE, HD)
        scores = jnp.einsum("tqd,tkd->tqk", query_tiles, key_sets.astype(jnp.float32)) * score_scale
        scores = jnp.where(allowed_keys[:, None, :], scores, -1e30)
        top_score = jnp.max(scores, axis=2, keepdims=True)
        exponent = jnp.where(allowed_keys[:, None, :], jnp.exp(scores - top_score), 0.0)
        weight_sum = jnp.sum(exponent, axis=2, keepdims=True)
        rounded = exponent.astype(jnp.bfloat16).astype(jnp.float32)
        mixed = jnp.einsum("tqk,tkd->tqd", rounded, value_sets.astype(jnp.float32))
        return (mixed / weight_sum).reshape(TOKENS, HD)

    def one_head(operands):
        kind_value, query_rows, key_rows, value_rows = operands
        result = lax.cond(kind_value == 1, global_head, tile_head, query_rows, key_rows, value_rows)
        return result.astype(jnp.bfloat16)

    attention = lax.map(one_head, (head_kind, query_heads, key_heads, value_heads))
    weight_heads = out_weight.reshape(HEADS, HD, D)
    projected = jnp.zeros((TOKENS, D), jnp.float32)
    for block_index in range(HEADS // HEADS_DEV):
        first_head = block_index * HEADS_DEV
        partial_sum = jnp.einsum("htd,hde->te", attention[first_head:first_head + HEADS_DEV].astype(jnp.float32), weight_heads[first_head:first_head + HEADS_DEV].astype(jnp.float32))
        projected = projected + partial_sum.astype(jnp.bfloat16).astype(jnp.float32)
    return projected.astype(jnp.bfloat16)
```

```python
import functools
import math

import jax
import jax.numpy as jnp
from jax import lax
from jax.experimental import pallas as pl
from jax.experimental.pallas import tpu as pltpu
from jax.sharding import PartitionSpec as P

MESH = pl.DeviceIdType.MESH
F32 = jnp.float32
BF16 = jnp.bfloat16

ROWS = 768
TILE = 384
HD = 128
D = 5120
CH = 2
CROWS = ROWS // CH
DROWS = CROWS // 8
ZROWS = 2 * DROWS
CA = 2816
CB = D - CA
HB = CB // 2
NEG = -1e30
OFF = -2e30
SCALE = HD**-0.5 * math.log2(math.e)


def dot(a, b, ca, cb):
    return lax.dot_general(a, b, (((ca,), (cb,)), ((), ())), preferred_element_type=F32)


def scores(q, k):
    scaled = q.astype(F32) * SCALE
    high = scaled.astype(BF16)
    low = (scaled - high.astype(F32)).astype(BF16)
    return dot(jnp.concatenate([high, low], axis=1), jnp.concatenate([k, k], axis=1), 1, 1)


def fold(s, v, bias, m, acc):
    tiles = len(bias)
    rows = s.shape[0]
    new = m
    for t in range(tiles):
        part = s[:, t * TILE : (t + 1) * TILE]
        top = jnp.broadcast_to(jnp.max(part, axis=1, keepdims=True), (rows, HD))
        new = jnp.maximum(new, top + bias[t])
    pieces = []
    for t in range(tiles):
        sub = new - bias[t]
        for u in range(TILE // HD):
            at = t * TILE + u * HD
            pieces.append(jnp.exp2(s[:, at : at + HD] - sub).astype(BF16))
    o = dot(jnp.concatenate(pieces, axis=1), jnp.concatenate([v, jnp.ones_like(v)], axis=1), 1, 0)
    if acc is None:
        return new, o
    f = jnp.exp2(m - new)
    return new, acc * jnp.concatenate([f, f], axis=1) + o


def kernel(
    kind_ref, near_ref, mask_ref, q_ref, kv_ref, w_hbm, out_ref,
    w_ref, qall, qslide, kbuf, wbuf, tsend, trecv, tab, m_ref, acc_ref,
    osend, lsend, orecv, lrecv, attn, pbuf,
    fa, ra, xa, xb, fb, rb,
    w_sem, q_ss, q_rs, t_ss, t_rs, kx_ss, kx_rs, kc_ss, kc_rs, h_ss, h_rs,
    o_ss, o_rs, l_ss, l_rs, r_ss, r_rs,
):
    frame = lax.axis_index("frame")
    head = lax.axis_index("head")
    xl, y, c = frame // 8, (frame // 2) % 4, frame % 2
    z, xh = head // 2, head % 2

    def frame_of(a, b, d):
        return (a * 4 + b) * 2 + d

    def at_y(g):
        return (frame_of(xl, (y + g) % 4, c), head)

    core = (frame_of(xl, y, 1 - c), head)
    across = (frame_of(1 - xl, y, c), head)
    after = ((frame + 1) % 16, head)
    before = ((frame + 15) % 16, head)
    z_up = (frame, ((z + 1) % 4) * 2 + xh)
    z_down = (frame, ((z + 3) % 4) * 2 + xh)
    x_other = (frame, z * 2 + 1 - xh)

    load_w = pltpu.make_async_copy(w_hbm, w_ref, w_sem)
    load_w.start()

    barrier = pltpu.get_barrier_semaphore()
    peers = [at_y(1), at_y(2), at_y(3), core, across, after, before, z_up, z_down, x_other]
    for peer in peers:
        pl.semaphore_signal(barrier, inc=1, device_id=peer, device_id_type=MESH)
    pl.semaphore_wait(barrier, len(peers))

    def remote(src, dst, ss, rs, peer):
        return pltpu.make_async_remote_copy(
            src_ref=src, dst_ref=dst, send_sem=ss, recv_sem=rs, device_id=peer, device_id_type=MESH
        )

    sent = []

    def start(copy):
        copy.start()
        sent.append(copy)
        return copy

    kinds = [kind_ref[i] for i in range(5)]
    many = functools.reduce(jnp.add, kinds)
    order = [0] * 5
    seen = 0
    for i in range(5):
        slot = jnp.where(kinds[i] == 1, seen, many + i - seen)
        seen = seen + kinds[i]
        order = [jnp.where(slot == s, i, order[s]) for s in range(5)]
    heads_of = [range(5), range(5), range(0, 3), range(1, 4), range(2, 5)]

    def choose(s, get):
        value = get(heads_of[s][0])
        for i in heads_of[s][1:]:
            value = lax.select(order[s] == i, get(i), value)
        return value

    @pl.loop(0, ROWS // 96)
    def _(r):
        rows = pl.ds(pl.multiple_of(r * 96, 96), 96)
        for s in range(2):
            for t in range(2):
                kbuf[0, s, t, rows, :] = choose(s, lambda i: kv_ref[t, i, rows, :])

    kx = [
        start(remote(kbuf.at[0, s, :, pl.ds(0, ROWS)], kbuf.at[1, s, :, pl.ds(0, ROWS)],
                     kx_ss.at[s], kx_rs.at[s], across))
        for s in range(2)
    ]
    kc = [
        [remote(kbuf.at[b, s, :, pl.ds(0, ROWS)], kbuf.at[b, s, :, pl.ds(ROWS, ROWS)],
                kc_ss.at[b, s], kc_rs.at[b, s], core) for s in range(2)]
        for b in range(2)
    ]
    for s in range(2):
        start(kc[0][s])
    def stage_queries(slots, store):
        for k in range(CH):

            @pl.loop(0, 8)
            def _(d):
                dest = ((z + d // 2) % 4) * 2 + (xh + d % 2) % 2
                rows = pl.ds(pl.multiple_of((dest * CH + k) * DROWS, 16), DROWS)
                to = pl.ds(pl.multiple_of(k * CROWS + d * DROWS, 16), DROWS)
                for s in slots:
                    store(s, to, choose(s, lambda i: q_ref[i, rows, :]))

    def store_temporal(s, to, value):
        qall[0, s, to, :] = value

    def store_sliding(s, to, value):
        qslide[s - 2, to, :] = value

    stage_queries(range(2), store_temporal)

    def allowed(half, ids):
        hit = ids == frame * 2 + half
        for n in range(2):
            listed = jnp.where(mask_ref[half, n] == 1, near_ref[half, n], -5)
            hit = hit | (ids == listed)
        return hit

    lane_ids = lax.broadcasted_iota(jnp.int32, (1, HD), 1)
    for s in range(2):
        shift = jnp.where(s < many, 0.0, OFF)
        for half in range(2):
            tsend[s * 2 + half : s * 2 + half + 1, :] = jnp.where(allowed(half, lane_ids), 0.0, shift)
    tsend[4:8, :] = jnp.zeros((4, HD), F32)
    window_ids = frame * 2 - 1 + lax.broadcasted_iota(jnp.int32, (8, HD), 0)
    window = [jnp.where(allowed(half, window_ids), 0.0, OFF) for half in range(2)]
    qx, tx = [None] * 4, [None] * 4
    for g in (1, 3, 2):
        tx[g] = start(remote(tsend, trecv.at[4 - g], t_ss.at[g], t_rs.at[4 - g], at_y(g)))
        qx[g] = start(remote(qall.at[0], qall.at[4 - g], q_ss.at[g], q_rs.at[4 - g], at_y(g)))

    @pl.loop(0, ROWS // 96)
    def _(r):
        rows = pl.ds(pl.multiple_of(r * 96, 96), 96)
        to = pl.ds(pl.multiple_of(TILE + r * 96, 96), 96)
        for s in range(3):
            for t in range(2):
                wbuf[s, t, to, :] = choose(s + 2, lambda i: kv_ref[t, i, rows, :])

    h_next = start(remote(wbuf.at[:, :, pl.ds(2 * TILE, TILE)], wbuf.at[:, :, pl.ds(0, TILE)],
                          h_ss.at[0], h_rs.at[0], after))
    h_prev = start(remote(wbuf.at[:, :, pl.ds(TILE, TILE)], wbuf.at[:, :, pl.ds(3 * TILE, TILE)],
                          h_ss.at[1], h_rs.at[1], before))

    def spread(src, g):
        for i in range(4):
            row = jnp.broadcast_to(src[i : i + 1, :], (128, 128))
            tab[g, i] = jnp.transpose(row)[0:32]

    spread(tsend[...], 0)
    stage_queries(range(2, 5), store_sliding)

    half_of = [((z + zr) % 4) // 2 for zr in range(4)]

    def rows_bias(get):
        low, high = get(0), get(1)
        blocks = []
        for zr in range(4):
            pick = jnp.where(half_of[zr] == 0, low, high)
            blocks.append(jnp.broadcast_to(pick, (ZROWS, HD)))
        return jnp.concatenate(blocks, axis=0)

    def temporal_bias(g, s, b):
        bias = []
        for d in range(2):
            part = frame_of(xl if b == 0 else 1 - xl, y, c if d == 0 else 1 - c)
            for t in range(2):
                bias.append(rows_bias(lambda half: tab[g, s * 2 + half, pl.ds(part * 2 + t, 1), :]))
        return bias

    def temporal(g, b, chunks, first):
        items = [(s, k) for s in range(2) for k in chunks]
        bias = [temporal_bias(g, s, b) for s in range(2)]

        def score(item):
            s, k = item
            return scores(qall[g, s, pl.ds(k * CROWS, CROWS), :], kbuf[b, s, 0])

        ahead = score(items[0])
        for i, (s, k) in enumerate(items):
            now = ahead
            if i + 1 < len(items):
                ahead = score(items[i + 1])
            rows = pl.ds(k * CROWS, CROWS)
            if first:
                m, acc = jnp.full((CROWS, HD), NEG, F32), None
            else:
                m, acc = m_ref[g, s, rows, :], acc_ref[g, s, rows, :]
            m, acc = fold(now, kbuf[b, s, 1], bias[s], m, acc)
            m_ref[g, s, rows, :] = m
            acc_ref[g, s, rows, :] = acc

    def send_o(g):
        for s in range(2):
            total = acc_ref[g, s, :, HD:]
            safe = jnp.where(total > 0, total, 1.0)
            osend[g, s] = (acc_ref[g, s, :, :HD] / safe).astype(BF16)
            log = m_ref[g, s] + jnp.log2(safe)
            lsend[g, s] = jnp.transpose(log)[0:8]

    def o_copies(g):
        return (
            remote(osend.at[g], orecv.at[4 - g], o_ss.at[g], o_rs.at[4 - g], at_y(g)),
            remote(lsend.at[g], lrecv.at[4 - g], l_ss.at[g], l_rs.at[4 - g], at_y(g)),
        )

    for s in range(2):
        kc[0][s].wait_recv()
    temporal(0, 0, range(CH), True)

    h_next.wait_recv()
    h_prev.wait_recv()

    window_bias = [
        rows_bias(lambda half, t=t: window[half][t : t + 1, :]) for t in range(4)
    ]
    items = [(s, k) for s in range(3) for k in range(CH)]
    ahead = scores(qslide[0, 0:CROWS, :], wbuf[0, 0])
    for i, (s, k) in enumerate(items):
        now = ahead
        if i + 1 < len(items):
            s1, k1 = items[i + 1]
            ahead = scores(qslide[s1, k1 * CROWS : (k1 + 1) * CROWS, :], wbuf[s1, 0])
        _, acc = fold(now, wbuf[s, 1], window_bias, jnp.full((CROWS, HD), NEG, F32), None)
        attn[k, :, (s + 2) * HD : (s + 3) * HD] = (acc[:, :HD] / acc[:, HD:]).astype(BF16)

    for g in (1, 3):
        tx[4 - g].wait_recv()
        qx[4 - g].wait_recv()
        spread(trecv[g], g)

    kx[0].wait_recv()
    start(kc[1][0])

    @pl.loop(0, 2)
    def _(i):
        temporal(1 + 2 * i, 0, range(CH), True)

    kx[1].wait_recv()
    start(kc[1][1])
    for s in range(2):
        kc[1][s].wait_recv()

    @pl.loop(0, 2)
    def _(i):
        g = 1 + 2 * i
        temporal(g, 1, range(CH), False)
        send_o(g)
        for copy in o_copies(g):
            copy.start()

    tx[2].wait_recv()
    qx[2].wait_recv()
    spread(trecv[2], 2)
    temporal(2, 0, range(CH), True)
    temporal(2, 1, range(CH), False)
    send_o(2)
    for copy in o_copies(2):
        copy.start()

    def combine(k):
        rows = pl.ds(k * CROWS, CROWS)
        for s in range(2):
            total = acc_ref[0, s, rows, HD:]
            logs = [m_ref[0, s, rows, :] + jnp.log2(total)]
            outs = [acc_ref[0, s, rows, :HD] / total]
            for g in range(1, 4):
                line = lrecv[g, s, 0:1, k * CROWS : (k + 1) * CROWS]
                logs.append(jnp.transpose(jnp.broadcast_to(line, (HD, CROWS))))
                outs.append(orecv[g, s, rows, :].astype(F32))
            top = functools.reduce(jnp.maximum, logs)
            weights = [jnp.exp2(log - top) for log in logs]
            mixed = functools.reduce(jnp.add, [w * o for w, o in zip(weights, outs)])
            attn[k, :, s * HD : (s + 1) * HD] = (
                mixed / functools.reduce(jnp.add, weights)
            ).astype(BF16)

    WIDTH = 512

    def project(k):
        slots = [attn[k, :, s * HD : (s + 1) * HD] for s in range(5)]
        for i in range(5):
            value = slots[0]
            for s in range(1, 5):
                if i in heads_of[s]:
                    value = lax.select(order[s] == i, slots[s], value)
            attn[k, :, i * HD : (i + 1) * HD] = value

        @pl.loop(0, D // WIDTH)
        def _(j):
            columns = pl.ds(pl.multiple_of(j * WIDTH, WIDTH), WIDTH)
            pbuf[k, :, columns] = dot(attn[k], w_ref[:, columns], 1, 0).astype(BF16)

    def block(k, zr, xr, first, width):
        return pbuf.at[k, pl.ds((zr * 2 + xr) * DROWS, DROWS), pl.ds(first, width)]

    def add(k, zr, xr, first, width, *others):
        @pl.loop(0, DROWS // 16)
        def _(i):
            rows = pl.ds(pl.multiple_of((zr * 2 + xr) * DROWS + i * 16, 16), 16)
            value = pbuf[k, rows, first : first + width].astype(F32)
            for other in others:
                value += other[pl.ds(pl.multiple_of(i * 16, 16), 16), :].astype(F32)
            pbuf[k, rows, first : first + width] = value.astype(BF16)

    def emit(k, first, width, *others):
        @pl.loop(0, DROWS // 16)
        def _(i):
            value = pbuf[k, pl.ds(pl.multiple_of(i * 16, 16), 16), first : first + width].astype(F32)
            for other in others:
                value += other[pl.ds(pl.multiple_of(i * 16, 16), 16), :].astype(F32)
            rows = pl.ds(pl.multiple_of(k * DROWS + i * 16, 16), 16)
            out_ref[rows, first : first + width] = value.astype(BF16)

    H1, H2 = CA, CA + HB

    class Chunk:
        def __init__(self, k):
            self.k = k
            self.count = 0

        def send(self, src, dst, peer):
            n = self.count
            self.count += 1
            return start(remote(src, dst, r_ss.at[self.k, n], r_rs.at[self.k, n], peer))

        def first(self):
            k = self.k
            self.fa = [
                self.send(block(k, 2, 0, 0, CA), fa.at[k, 0], z_up),
                self.send(block(k, 2, 1, 0, CA), fa.at[k, 1], z_down),
            ]
            self.xb = {}
            for zr in (2, 1, 3, 0):
                self.xb[zr] = self.send(block(k, zr, 1, CA, CB), xb.at[k, zr], x_other)
            self.ra = [
                self.send(block(k, 1, 1, 0, CA), ra.at[k, 0, 1], z_up),
                self.send(block(k, 3, 0, 0, CA), ra.at[k, 1, 0], z_down),
            ]

        def forward_a(self):
            k = self.k
            self.fa[0].wait_recv()
            add(k, 1, 0, 0, CA, fa.at[k, 0])
            self.ra.append(self.send(block(k, 1, 0, 0, CA), ra.at[k, 0, 0], z_up))
            self.fa[1].wait_recv()
            add(k, 3, 1, 0, CA, fa.at[k, 1])
            self.ra.append(self.send(block(k, 3, 1, 0, CA), ra.at[k, 1, 1], z_down))

        def second_b(self):
            k = self.k
            self.xb[2].wait_recv()
            add(k, 2, 0, CA, CB, xb.at[k, 2])
            self.fb = [
                self.send(block(k, 2, 0, H1, HB), fb.at[k, 0], z_up),
                self.send(block(k, 2, 0, H2, HB), fb.at[k, 1], z_down),
            ]
            self.xb[1].wait_recv()
            add(k, 1, 0, CA, CB, xb.at[k, 1])
            self.rb = [self.send(block(k, 1, 0, H2, HB), rb.at[k, 0, 1], z_up)]
            self.xb[3].wait_recv()
            add(k, 3, 0, CA, CB, xb.at[k, 3])
            self.rb.append(self.send(block(k, 3, 0, H1, HB), rb.at[k, 1, 0], z_down))

        def third_a(self):
            k = self.k
            for copy in self.ra:
                copy.wait_recv()
            add(k, 0, 1, 0, CA, ra.at[k, 0, 1], ra.at[k, 1, 1])
            self.xa = self.send(block(k, 0, 1, 0, CA), xa.at[k], x_other)

        def forward_b(self):
            k = self.k
            self.fb[0].wait_recv()
            add(k, 1, 0, H1, HB, fb.at[k, 0])
            self.rb.append(self.send(block(k, 1, 0, H1, HB), rb.at[k, 0, 0], z_up))
            self.fb[1].wait_recv()
            add(k, 3, 0, H2, HB, fb.at[k, 1])
            self.rb.append(self.send(block(k, 3, 0, H2, HB), rb.at[k, 1, 1], z_down))

        def finish(self):
            k = self.k
            self.xa.wait_recv()
            emit(k, 0, CA, ra.at[k, 0, 0], ra.at[k, 1, 0], xa.at[k])
            self.xb[0].wait_recv()
            for copy in self.rb:
                copy.wait_recv()
            emit(k, H1, HB, xb.at[k, 0, :, pl.ds(0, HB)], rb.at[k, 0, 0], rb.at[k, 1, 0])
            emit(k, H2, HB, xb.at[k, 0, :, pl.ds(HB, HB)], rb.at[k, 0, 1], rb.at[k, 1, 1])

    one, two = Chunk(0), Chunk(1)
    temporal(0, 1, [0], False)
    for g in (1, 3, 2):
        for copy in o_copies(4 - g):
            copy.wait_recv()
    combine(0)
    load_w.wait()
    project(0)
    one.first()
    temporal(0, 1, [1], False)
    combine(1)
    one.forward_a()
    project(1)
    two.first()
    one.second_b()
    two.forward_a()
    one.third_a()
    one.forward_b()
    two.second_b()
    two.third_a()
    two.forward_b()
    one.finish()
    two.finish()

    for copy in sent:
        copy.wait_send()
    for g in range(1, 4):
        for copy in o_copies(g):
            copy.wait_send()


def per_device(queries, keys_values, head_kind, tile_neighbours, tile_mask, out_weight):
    smem = pl.BlockSpec(memory_space=pltpu.SMEM)
    vmem = pl.BlockSpec(memory_space=pltpu.VMEM)
    dma = pltpu.SemaphoreType.DMA
    return pl.pallas_call(
        kernel,
        out_shape=jax.ShapeDtypeStruct((ROWS // 8, D), BF16),
        in_specs=[
            smem, smem, smem,
            vmem, vmem,
            pl.BlockSpec(memory_space=pl.ANY),
        ],
        out_specs=vmem,
        scratch_shapes=[
            pltpu.VMEM((5 * HD, D), BF16),
            pltpu.VMEM((4, 2, ROWS, HD), BF16),
            pltpu.VMEM((3, ROWS, HD), BF16),
            pltpu.VMEM((2, 2, 2, 2 * ROWS, HD), BF16),
            pltpu.VMEM((3, 2, 4 * TILE, HD), BF16),
            pltpu.VMEM((8, HD), F32),
            pltpu.VMEM((4, 8, HD), F32),
            pltpu.VMEM((4, 4, 32, HD), F32),
            pltpu.VMEM((4, 2, ROWS, HD), F32),
            pltpu.VMEM((4, 2, ROWS, 2 * HD), F32),
            pltpu.VMEM((4, 2, ROWS, HD), BF16),
            pltpu.VMEM((4, 2, 8, ROWS), F32),
            pltpu.VMEM((4, 2, ROWS, HD), BF16),
            pltpu.VMEM((4, 2, 8, ROWS), F32),
            pltpu.VMEM((CH, CROWS, 5 * HD), BF16),
            pltpu.VMEM((CH, CROWS, D), BF16),
            pltpu.VMEM((CH, 2, DROWS, CA), BF16),
            pltpu.VMEM((CH, 2, 2, DROWS, CA), BF16),
            pltpu.VMEM((CH, DROWS, CA), BF16),
            pltpu.VMEM((CH, 4, DROWS, CB), BF16),
            pltpu.VMEM((CH, 2, DROWS, HB), BF16),
            pltpu.VMEM((CH, 2, 2, DROWS, HB), BF16),
            dma,
            dma((4,)), dma((4,)),
            dma((4,)), dma((4,)),
            dma((2,)), dma((2,)),
            dma((2, 2)), dma((2, 2)),
            dma((2,)), dma((2,)),
            dma((4,)), dma((4,)),
            dma((4,)), dma((4,)),
            dma((CH, 20)), dma((CH, 20)),
        ],
        name="attend_project",
        compiler_params=pltpu.CompilerParams(
            collective_id=0, has_side_effects=True, vmem_limit_bytes=60 * 2**20
        ),
    )(
        head_kind,
        tile_neighbours,
        tile_mask,
        jnp.transpose(queries, (1, 0, 2)),
        jnp.transpose(keys_values, (0, 2, 1, 3)),
        out_weight,
    )


def solution(mesh):
    return jax.shard_map(
        per_device,
        mesh=mesh,
        in_specs=(
            P("frame", "head", None),
            P(None, "frame", "head", None),
            P("head"),
            P("frame", None),
            P("frame", None),
            P("head", None),
        ),
        out_specs=P(("frame", "head"), None),
        check_vma=False,
    )
```

```python
import functools
import math

import jax
import jax.numpy as jnp
from jax import lax
from jax.experimental import pallas as pl
from jax.experimental.pallas import tpu as pltpu
from jax.sharding import PartitionSpec as P

MESH = pl.DeviceIdType.MESH
F32 = jnp.float32
BF16 = jnp.bfloat16

ROWS = 768
TILE = 384
HD = 128
D = 5120
CH = 2
CROWS = ROWS // CH
DROWS = CROWS // 8
ZROWS = 2 * DROWS
CA = 2816
CB = D - CA
HB = CB // 2
NEG = -1e30
OFF = -2e30
SCALE = HD**-0.5 * math.log2(math.e)


def dot(a, b, ca, cb):
    return lax.dot_general(a, b, (((ca,), (cb,)), ((), ())), preferred_element_type=F32)


def scores(q, k):
    scaled = q.astype(F32) * SCALE
    high = scaled.astype(BF16)
    low = (scaled - high.astype(F32)).astype(BF16)
    return dot(jnp.concatenate([high, low], axis=1), jnp.concatenate([k, k], axis=1), 1, 1)


def fold(s, v, bias, m, acc):
    tiles = len(bias)
    rows = s.shape[0]
    new = m
    for t in range(tiles):
        part = s[:, t * TILE : (t + 1) * TILE]
        top = jnp.broadcast_to(jnp.max(part, axis=1, keepdims=True), (rows, HD))
        new = jnp.maximum(new, top + bias[t])
    pieces = []
    for t in range(tiles):
        sub = new - bias[t]
        for u in range(TILE // HD):
            at = t * TILE + u * HD
            pieces.append(jnp.exp2(s[:, at : at + HD] - sub).astype(BF16))
    o = dot(jnp.concatenate(pieces, axis=1), jnp.concatenate([v, jnp.ones_like(v)], axis=1), 1, 0)
    if acc is None:
        return new, o
    f = jnp.exp2(m - new)
    return new, acc * jnp.concatenate([f, f], axis=1) + o


def kernel(
    kind_ref, near_ref, mask_ref, q_ref, kv_ref, w_hbm, out_ref,
    w_ref, qall, qslide, kbuf, wbuf, tsend, trecv, tab, m_ref, acc_ref,
    osend, lsend, orecv, lrecv, attn, pbuf,
    fa, ra, xa, xb, fb, rb,
    w_sem, q_ss, q_rs, t_ss, t_rs, kx_ss, kx_rs, kc_ss, kc_rs, h_ss, h_rs,
    o_ss, o_rs, l_ss, l_rs, r_ss, r_rs,
):
    frame = lax.axis_index("frame")
    head = lax.axis_index("head")
    xl, y, c = frame // 8, (frame // 2) % 4, frame % 2
    z, xh = head // 2, head % 2

    def frame_of(a, b, d):
        return (a * 4 + b) * 2 + d

    def at_y(g):
        return (frame_of(xl, (y + g) % 4, c), head)

    core = (frame_of(xl, y, 1 - c), head)
    across = (frame_of(1 - xl, y, c), head)
    after = ((frame + 1) % 16, head)
    before = ((frame + 15) % 16, head)
    z_up = (frame, ((z + 1) % 4) * 2 + xh)
    z_down = (frame, ((z + 3) % 4) * 2 + xh)
    x_other = (frame, z * 2 + 1 - xh)

    load_w = pltpu.make_async_copy(w_hbm, w_ref, w_sem)
    load_w.start()

    barrier = pltpu.get_barrier_semaphore()
    peers = [at_y(1), at_y(2), at_y(3), core, across, after, before, z_up, z_down, x_other]
    for peer in peers:
        pl.semaphore_signal(barrier, inc=1, device_id=peer, device_id_type=MESH)
    pl.semaphore_wait(barrier, len(peers))

    def remote(src, dst, ss, rs, peer):
        return pltpu.make_async_remote_copy(
            src_ref=src, dst_ref=dst, send_sem=ss, recv_sem=rs, device_id=peer, device_id_type=MESH
        )

    sent = []

    def start(copy):
        copy.start()
        sent.append(copy)
        return copy

    kinds = [kind_ref[i] for i in range(5)]
    many = functools.reduce(jnp.add, kinds)
    order = [0] * 5
    seen = 0
    for i in range(5):
        slot = jnp.where(kinds[i] == 1, seen, many + i - seen)
        seen = seen + kinds[i]
        order = [jnp.where(slot == s, i, order[s]) for s in range(5)]
    heads_of = [range(5), range(5), range(0, 3), range(1, 4), range(2, 5)]

    def choose(s, get):
        value = get(heads_of[s][0])
        for i in heads_of[s][1:]:
            value = lax.select(order[s] == i, get(i), value)
        return value

    @pl.loop(0, ROWS // 96)
    def _(r):
        rows = pl.ds(pl.multiple_of(r * 96, 96), 96)
        for s in range(2):
            for t in range(2):
                kbuf[0, s, t, rows, :] = choose(s, lambda i: kv_ref[t, i, rows, :])

    kx = [
        start(remote(kbuf.at[0, s, :, pl.ds(0, ROWS)], kbuf.at[1, s, :, pl.ds(0, ROWS)],
                     kx_ss.at[s], kx_rs.at[s], across))
        for s in range(2)
    ]
    kc = [
        [remote(kbuf.at[b, s, :, pl.ds(0, ROWS)], kbuf.at[b, s, :, pl.ds(ROWS, ROWS)],
                kc_ss.at[b, s], kc_rs.at[b, s], core) for s in range(2)]
        for b in range(2)
    ]
    for s in range(2):
        start(kc[0][s])
    def stage_queries(slots, store):
        for k in range(CH):

            @pl.loop(0, 8)
            def _(d):
                dest = ((z + d // 2) % 4) * 2 + (xh + d % 2) % 2
                rows = pl.ds(pl.multiple_of((dest * CH + k) * DROWS, 16), DROWS)
                to = pl.ds(pl.multiple_of(k * CROWS + d * DROWS, 16), DROWS)
                for s in slots:
                    store(s, to, choose(s, lambda i: q_ref[i, rows, :]))

    def store_temporal(s, to, value):
        qall[0, s, to, :] = value

    def store_sliding(s, to, value):
        qslide[s - 2, to, :] = value

    stage_queries(range(2), store_temporal)

    def allowed(half, ids):
        hit = ids == frame * 2 + half
        for n in range(2):
            listed = jnp.where(mask_ref[half, n] == 1, near_ref[half, n], -5)
            hit = hit | (ids == listed)
        return hit

    lane_ids = lax.broadcasted_iota(jnp.int32, (1, HD), 1)
    for s in range(2):
        shift = jnp.where(s < many, 0.0, OFF)
        for half in range(2):
            tsend[s * 2 + half : s * 2 + half + 1, :] = jnp.where(allowed(half, lane_ids), 0.0, shift)
    tsend[4:8, :] = jnp.zeros((4, HD), F32)
    window_ids = frame * 2 - 1 + lax.broadcasted_iota(jnp.int32, (8, HD), 0)
    window = [jnp.where(allowed(half, window_ids), 0.0, OFF) for half in range(2)]
    qx, tx = [None] * 4, [None] * 4
    for g in (1, 3, 2):
        tx[g] = start(remote(tsend, trecv.at[4 - g], t_ss.at[g], t_rs.at[4 - g], at_y(g)))
        qx[g] = start(remote(qall.at[0], qall.at[4 - g], q_ss.at[g], q_rs.at[4 - g], at_y(g)))

    @pl.loop(0, ROWS // 96)
    def _(r):
        rows = pl.ds(pl.multiple_of(r * 96, 96), 96)
        to = pl.ds(pl.multiple_of(TILE + r * 96, 96), 96)
        for s in range(3):
            for t in range(2):
                wbuf[s, t, to, :] = choose(s + 2, lambda i: kv_ref[t, i, rows, :])

    h_next = start(remote(wbuf.at[:, :, pl.ds(2 * TILE, TILE)], wbuf.at[:, :, pl.ds(0, TILE)],
                          h_ss.at[0], h_rs.at[0], after))
    h_prev = start(remote(wbuf.at[:, :, pl.ds(TILE, TILE)], wbuf.at[:, :, pl.ds(3 * TILE, TILE)],
                          h_ss.at[1], h_rs.at[1], before))

    def spread(src, g):
        for i in range(4):
            row = jnp.broadcast_to(src[i : i + 1, :], (128, 128))
            tab[g, i] = jnp.transpose(row)[0:32]

    spread(tsend[...], 0)
    stage_queries(range(2, 5), store_sliding)

    half_of = [((z + zr) % 4) // 2 for zr in range(4)]

    def rows_bias(get):
        low, high = get(0), get(1)
        blocks = []
        for zr in range(4):
            pick = jnp.where(half_of[zr] == 0, low, high)
            blocks.append(jnp.broadcast_to(pick, (ZROWS, HD)))
        return jnp.concatenate(blocks, axis=0)

    def temporal_bias(g, s, b):
        bias = []
        for d in range(2):
            part = frame_of(xl if b == 0 else 1 - xl, y, c if d == 0 else 1 - c)
            for t in range(2):
                bias.append(rows_bias(lambda half: tab[g, s * 2 + half, pl.ds(part * 2 + t, 1), :]))
        return bias

    def temporal(g, b, chunks, first, done=None):
        items = [(s, k) for s in range(2) for k in chunks]
        bias = [temporal_bias(g, s, b) for s in range(2)]

        def score(item):
            s, k = item
            return scores(qall[g, s, pl.ds(k * CROWS, CROWS), :], kbuf[b, s, 0])

        ahead = score(items[0])
        for i, (s, k) in enumerate(items):
            now = ahead
            if i + 1 < len(items):
                ahead = score(items[i + 1])
            rows = pl.ds(k * CROWS, CROWS)
            if first:
                m, acc = jnp.full((CROWS, HD), NEG, F32), None
            else:
                m, acc = m_ref[g, s, rows, :], acc_ref[g, s, rows, :]
            m, acc = fold(now, kbuf[b, s, 1], bias[s], m, acc)
            m_ref[g, s, rows, :] = m
            acc_ref[g, s, rows, :] = acc
            if done is not None and k == CH - 1:
                done(s)

    def o_copies(g, s):
        return (
            remote(osend.at[g, s], orecv.at[4 - g, s], o_ss.at[g, s], o_rs.at[4 - g, s], at_y(g)),
            remote(lsend.at[g, s], lrecv.at[4 - g, s], l_ss.at[g, s], l_rs.at[4 - g, s], at_y(g)),
        )

    def send_o(g, s):
        total = acc_ref[g, s, :, HD:]
        safe = jnp.where(total > 0, total, 1.0)
        osend[g, s] = (acc_ref[g, s, :, :HD] / safe).astype(BF16)
        log = m_ref[g, s] + jnp.log2(safe)
        lsend[g, s] = jnp.transpose(log)[0:8]
        for copy in o_copies(g, s):
            copy.start()

    def arrived(g):
        tx[4 - g].wait_recv()
        qx[4 - g].wait_recv()
        spread(trecv[g], g)

    for s in range(2):
        kc[0][s].wait_recv()
    temporal(0, 0, range(CH), True)
    arrived(1)
    temporal(1, 0, range(CH), True)
    kx[0].wait_recv()
    start(kc[1][0])
    arrived(3)
    temporal(3, 0, range(CH), True)
    kx[1].wait_recv()
    start(kc[1][1])
    for s in range(2):
        kc[1][s].wait_recv()

    @pl.loop(0, 2)
    def _(i):
        g = 1 + 2 * i
        temporal(g, 1, range(CH), False)
        for s in range(2):
            send_o(g, s)

    arrived(2)
    temporal(2, 0, range(CH), True)
    temporal(2, 1, range(CH), False, lambda s: send_o(2, s))
    temporal(0, 1, range(CH), False)

    h_next.wait_recv()
    h_prev.wait_recv()

    window_bias = [
        rows_bias(lambda half, t=t: window[half][t : t + 1, :]) for t in range(4)
    ]
    items = [(s, k) for s in range(3) for k in range(CH)]
    ahead = scores(qslide[0, 0:CROWS, :], wbuf[0, 0])
    for i, (s, k) in enumerate(items):
        now = ahead
        if i + 1 < len(items):
            s1, k1 = items[i + 1]
            ahead = scores(qslide[s1, k1 * CROWS : (k1 + 1) * CROWS, :], wbuf[s1, 0])
        _, acc = fold(now, wbuf[s, 1], window_bias, jnp.full((CROWS, HD), NEG, F32), None)
        attn[k, :, (s + 2) * HD : (s + 3) * HD] = (acc[:, :HD] / acc[:, HD:]).astype(BF16)

    def combine(k):
        rows = pl.ds(k * CROWS, CROWS)
        for s in range(2):
            total = acc_ref[0, s, rows, HD:]
            logs = [m_ref[0, s, rows, :] + jnp.log2(total)]
            outs = [acc_ref[0, s, rows, :HD] / total]
            for g in range(1, 4):
                line = lrecv[g, s, 0:1, k * CROWS : (k + 1) * CROWS]
                logs.append(jnp.transpose(jnp.broadcast_to(line, (HD, CROWS))))
                outs.append(orecv[g, s, rows, :].astype(F32))
            top = functools.reduce(jnp.maximum, logs)
            weights = [jnp.exp2(log - top) for log in logs]
            mixed = functools.reduce(jnp.add, [w * o for w, o in zip(weights, outs)])
            attn[k, :, s * HD : (s + 1) * HD] = (
                mixed / functools.reduce(jnp.add, weights)
            ).astype(BF16)

    WIDTH = 512

    def project(k):
        slots = [attn[k, :, s * HD : (s + 1) * HD] for s in range(5)]
        for i in range(5):
            value = slots[0]
            for s in range(1, 5):
                if i in heads_of[s]:
                    value = lax.select(order[s] == i, slots[s], value)
            attn[k, :, i * HD : (i + 1) * HD] = value

        @pl.loop(0, D // WIDTH)
        def _(j):
            columns = pl.ds(pl.multiple_of(j * WIDTH, WIDTH), WIDTH)
            pbuf[k, :, columns] = dot(attn[k], w_ref[:, columns], 1, 0).astype(BF16)

    def block(k, zr, xr, first, width):
        return pbuf.at[k, pl.ds((zr * 2 + xr) * DROWS, DROWS), pl.ds(first, width)]

    def add(k, zr, xr, first, width, *others):
        @pl.loop(0, DROWS // 16)
        def _(i):
            rows = pl.ds(pl.multiple_of((zr * 2 + xr) * DROWS + i * 16, 16), 16)
            value = pbuf[k, rows, first : first + width].astype(F32)
            for other in others:
                value += other[pl.ds(pl.multiple_of(i * 16, 16), 16), :].astype(F32)
            pbuf[k, rows, first : first + width] = value.astype(BF16)

    def emit(k, first, width, *others):
        @pl.loop(0, DROWS // 16)
        def _(i):
            value = pbuf[k, pl.ds(pl.multiple_of(i * 16, 16), 16), first : first + width].astype(F32)
            for other in others:
                value += other[pl.ds(pl.multiple_of(i * 16, 16), 16), :].astype(F32)
            rows = pl.ds(pl.multiple_of(k * DROWS + i * 16, 16), 16)
            out_ref[rows, first : first + width] = value.astype(BF16)

    H1, H2 = CA, CA + HB

    class Chunk:
        def __init__(self, k):
            self.k = k
            self.count = 0

        def send(self, src, dst, peer):
            n = self.count
            self.count += 1
            return start(remote(src, dst, r_ss.at[self.k, n], r_rs.at[self.k, n], peer))

        def first(self):
            k = self.k
            self.fa = [
                self.send(block(k, 2, 0, 0, CA), fa.at[k, 0], z_up),
                self.send(block(k, 2, 1, 0, CA), fa.at[k, 1], z_down),
            ]
            self.xb = {}
            for zr in (2, 1, 3, 0):
                self.xb[zr] = self.send(block(k, zr, 1, CA, CB), xb.at[k, zr], x_other)
            self.ra = [
                self.send(block(k, 1, 1, 0, CA), ra.at[k, 0, 1], z_up),
                self.send(block(k, 3, 0, 0, CA), ra.at[k, 1, 0], z_down),
            ]

        def forward_a(self):
            k = self.k
            self.fa[0].wait_recv()
            add(k, 1, 0, 0, CA, fa.at[k, 0])
            self.ra.append(self.send(block(k, 1, 0, 0, CA), ra.at[k, 0, 0], z_up))
            self.fa[1].wait_recv()
            add(k, 3, 1, 0, CA, fa.at[k, 1])
            self.ra.append(self.send(block(k, 3, 1, 0, CA), ra.at[k, 1, 1], z_down))

        def second_b(self):
            k = self.k
            self.xb[2].wait_recv()
            add(k, 2, 0, CA, CB, xb.at[k, 2])
            self.fb = [
                self.send(block(k, 2, 0, H1, HB), fb.at[k, 0], z_up),
                self.send(block(k, 2, 0, H2, HB), fb.at[k, 1], z_down),
            ]
            self.xb[1].wait_recv()
            add(k, 1, 0, CA, CB, xb.at[k, 1])
            self.rb = [self.send(block(k, 1, 0, H2, HB), rb.at[k, 0, 1], z_up)]
            self.xb[3].wait_recv()
            add(k, 3, 0, CA, CB, xb.at[k, 3])
            self.rb.append(self.send(block(k, 3, 0, H1, HB), rb.at[k, 1, 0], z_down))

        def third_a(self):
            k = self.k
            for copy in self.ra:
                copy.wait_recv()
            add(k, 0, 1, 0, CA, ra.at[k, 0, 1], ra.at[k, 1, 1])
            self.xa = self.send(block(k, 0, 1, 0, CA), xa.at[k], x_other)

        def forward_b(self):
            k = self.k
            self.fb[0].wait_recv()
            add(k, 1, 0, H1, HB, fb.at[k, 0])
            self.rb.append(self.send(block(k, 1, 0, H1, HB), rb.at[k, 0, 0], z_up))
            self.fb[1].wait_recv()
            add(k, 3, 0, H2, HB, fb.at[k, 1])
            self.rb.append(self.send(block(k, 3, 0, H2, HB), rb.at[k, 1, 1], z_down))

        def finish(self):
            k = self.k
            self.xa.wait_recv()
            emit(k, 0, CA, ra.at[k, 0, 0], ra.at[k, 1, 0], xa.at[k])
            self.xb[0].wait_recv()
            for copy in self.rb:
                copy.wait_recv()
            emit(k, H1, HB, xb.at[k, 0, :, pl.ds(0, HB)], rb.at[k, 0, 0], rb.at[k, 1, 0])
            emit(k, H2, HB, xb.at[k, 0, :, pl.ds(HB, HB)], rb.at[k, 0, 1], rb.at[k, 1, 1])

    one, two = Chunk(0), Chunk(1)
    for g in (1, 3, 2):
        for s in range(2):
            for copy in o_copies(4 - g, s):
                copy.wait_recv()
    combine(0)
    load_w.wait()
    project(0)
    one.first()
    combine(1)
    project(1)
    two.first()
    one.forward_a()
    one.second_b()
    two.forward_a()
    one.third_a()
    one.forward_b()
    two.second_b()
    two.third_a()
    two.forward_b()
    one.finish()
    two.finish()

    for copy in sent:
        copy.wait_send()
    for g in range(1, 4):
        for s in range(2):
            for copy in o_copies(g, s):
                copy.wait_send()


def per_device(queries, keys_values, head_kind, tile_neighbours, tile_mask, out_weight):
    smem = pl.BlockSpec(memory_space=pltpu.SMEM)
    vmem = pl.BlockSpec(memory_space=pltpu.VMEM)
    dma = pltpu.SemaphoreType.DMA
    return pl.pallas_call(
        kernel,
        out_shape=jax.ShapeDtypeStruct((ROWS // 8, D), BF16),
        in_specs=[
            smem, smem, smem,
            vmem, vmem,
            pl.BlockSpec(memory_space=pl.ANY),
        ],
        out_specs=vmem,
        scratch_shapes=[
            pltpu.VMEM((5 * HD, D), BF16),
            pltpu.VMEM((4, 2, ROWS, HD), BF16),
            pltpu.VMEM((3, ROWS, HD), BF16),
            pltpu.VMEM((2, 2, 2, 2 * ROWS, HD), BF16),
            pltpu.VMEM((3, 2, 4 * TILE, HD), BF16),
            pltpu.VMEM((8, HD), F32),
            pltpu.VMEM((4, 8, HD), F32),
            pltpu.VMEM((4, 4, 32, HD), F32),
            pltpu.VMEM((4, 2, ROWS, HD), F32),
            pltpu.VMEM((4, 2, ROWS, 2 * HD), F32),
            pltpu.VMEM((4, 2, ROWS, HD), BF16),
            pltpu.VMEM((4, 2, 8, ROWS), F32),
            pltpu.VMEM((4, 2, ROWS, HD), BF16),
            pltpu.VMEM((4, 2, 8, ROWS), F32),
            pltpu.VMEM((CH, CROWS, 5 * HD), BF16),
            pltpu.VMEM((CH, CROWS, D), BF16),
            pltpu.VMEM((CH, 2, DROWS, CA), BF16),
            pltpu.VMEM((CH, 2, 2, DROWS, CA), BF16),
            pltpu.VMEM((CH, DROWS, CA), BF16),
            pltpu.VMEM((CH, 4, DROWS, CB), BF16),
            pltpu.VMEM((CH, 2, DROWS, HB), BF16),
            pltpu.VMEM((CH, 2, 2, DROWS, HB), BF16),
            dma,
            dma((4,)), dma((4,)),
            dma((4,)), dma((4,)),
            dma((2,)), dma((2,)),
            dma((2, 2)), dma((2, 2)),
            dma((2,)), dma((2,)),
            dma((4, 2)), dma((4, 2)),
            dma((4, 2)), dma((4, 2)),
            dma((CH, 20)), dma((CH, 20)),
        ],
        name="attend_project",
        compiler_params=pltpu.CompilerParams(
            collective_id=0, has_side_effects=True, vmem_limit_bytes=60 * 2**20
        ),
    )(
        head_kind,
        tile_neighbours,
        tile_mask,
        jnp.transpose(queries, (1, 0, 2)),
        jnp.transpose(keys_values, (0, 2, 1, 3)),
        out_weight,
    )


def solution(mesh):
    return jax.shard_map(
        per_device,
        mesh=mesh,
        in_specs=(
            P("frame", "head", None),
            P(None, "frame", "head", None),
            P("head"),
            P("frame", None),
            P("frame", None),
            P("head", None),
        ),
        out_specs=P(("frame", "head"), None),
        check_vma=False,
    )
```

```python
import functools
import math

import jax
import jax.numpy as jnp
from jax import lax
from jax.experimental import pallas as pl
from jax.experimental.pallas import tpu as pltpu
from jax.sharding import PartitionSpec as P

MESH = pl.DeviceIdType.MESH
F32 = jnp.float32
BF16 = jnp.bfloat16

ROWS = 768
TILE = 384
HD = 128
D = 5120
CH = 2
CROWS = ROWS // CH
DROWS = CROWS // 8
ZROWS = 2 * DROWS
CA = 2816
CB = D - CA
HB = CB // 2
NEG = -1e30
OFF = -2e30
SCALE = HD**-0.5 * math.log2(math.e)


def dot(a, b, ca, cb):
    return lax.dot_general(a, b, (((ca,), (cb,)), ((), ())), preferred_element_type=F32)


def scores(q, k):
    scaled = q.astype(F32) * SCALE
    high = scaled.astype(BF16)
    low = (scaled - high.astype(F32)).astype(BF16)
    return dot(jnp.concatenate([high, low], axis=1), jnp.concatenate([k, k], axis=1), 1, 1)


def fold(s, v, bias, m, acc):
    tiles = len(bias)
    rows = s.shape[0]
    new = m
    for t in range(tiles):
        part = s[:, t * TILE : (t + 1) * TILE]
        top = jnp.broadcast_to(jnp.max(part, axis=1, keepdims=True), (rows, HD))
        new = jnp.maximum(new, top + bias[t])
    pieces = []
    for t in range(tiles):
        sub = new - bias[t]
        for u in range(TILE // HD):
            at = t * TILE + u * HD
            pieces.append(jnp.exp2(s[:, at : at + HD] - sub).astype(BF16))
    o = dot(jnp.concatenate(pieces, axis=1), jnp.concatenate([v, jnp.ones_like(v)], axis=1), 1, 0)
    if acc is None:
        return new, o
    f = jnp.exp2(m - new)
    return new, acc * jnp.concatenate([f, f], axis=1) + o


def kernel(
    kind_ref, near_ref, mask_ref, q_ref, kv_ref, w_hbm, out_ref,
    w_ref, qall, qslide, kbuf, wbuf, tsend, trecv, tab, m_ref, acc_ref,
    osend, lsend, orecv, lrecv, attn, pbuf,
    fa, ra, xa, xb, fb, rb,
    w_sem, q_ss, q_rs, t_ss, t_rs, kx_ss, kx_rs, kc_ss, kc_rs, h_ss, h_rs,
    o_ss, o_rs, l_ss, l_rs, r_ss, r_rs,
):
    frame = lax.axis_index("frame")
    head = lax.axis_index("head")
    xl, y, c = frame // 8, (frame // 2) % 4, frame % 2
    z, xh = head // 2, head % 2

    def frame_of(a, b, d):
        return (a * 4 + b) * 2 + d

    def at_y(g):
        return (frame_of(xl, (y + g) % 4, c), head)

    core = (frame_of(xl, y, 1 - c), head)
    across = (frame_of(1 - xl, y, c), head)
    after = ((frame + 1) % 16, head)
    before = ((frame + 15) % 16, head)
    z_up = (frame, ((z + 1) % 4) * 2 + xh)
    z_down = (frame, ((z + 3) % 4) * 2 + xh)
    x_other = (frame, z * 2 + 1 - xh)

    load_w = pltpu.make_async_copy(w_hbm, w_ref, w_sem)
    load_w.start()

    barrier = pltpu.get_barrier_semaphore()
    peers = [at_y(1), at_y(2), at_y(3), core, across, after, before, z_up, z_down, x_other]
    for peer in peers:
        pl.semaphore_signal(barrier, inc=1, device_id=peer, device_id_type=MESH)
    pl.semaphore_wait(barrier, len(peers))

    def remote(src, dst, ss, rs, peer):
        return pltpu.make_async_remote_copy(
            src_ref=src, dst_ref=dst, send_sem=ss, recv_sem=rs, device_id=peer, device_id_type=MESH
        )

    sent = []

    def start(copy):
        copy.start()
        sent.append(copy)
        return copy

    kinds = [kind_ref[i] for i in range(5)]
    many = functools.reduce(jnp.add, kinds)
    order = [0] * 5
    seen = 0
    for i in range(5):
        slot = jnp.where(kinds[i] == 1, seen, many + i - seen)
        seen = seen + kinds[i]
        order = [jnp.where(slot == s, i, order[s]) for s in range(5)]
    heads_of = [range(5), range(5), range(0, 3), range(1, 4), range(2, 5)]

    def choose(s, get):
        value = get(heads_of[s][0])
        for i in heads_of[s][1:]:
            value = lax.select(order[s] == i, get(i), value)
        return value

    @pl.loop(0, ROWS // 96)
    def _(r):
        rows = pl.ds(pl.multiple_of(r * 96, 96), 96)
        for s in range(2):
            for t in range(2):
                kbuf[0, s, t, rows, :] = choose(s, lambda i: kv_ref[t, i, rows, :])

    kx = [
        start(remote(kbuf.at[0, s, :, pl.ds(0, ROWS)], kbuf.at[1, s, :, pl.ds(0, ROWS)],
                     kx_ss.at[s], kx_rs.at[s], across))
        for s in range(2)
    ]
    kc = [
        [remote(kbuf.at[b, s, :, pl.ds(0, ROWS)], kbuf.at[b, s, :, pl.ds(ROWS, ROWS)],
                kc_ss.at[b, s], kc_rs.at[b, s], core) for s in range(2)]
        for b in range(2)
    ]
    for s in range(2):
        start(kc[0][s])
    def stage_queries(slots, store):
        for k in range(CH):

            @pl.loop(0, 8)
            def _(d):
                dest = ((z + d // 2) % 4) * 2 + (xh + d % 2) % 2
                rows = pl.ds(pl.multiple_of((dest * CH + k) * DROWS, 16), DROWS)
                to = pl.ds(pl.multiple_of(k * CROWS + d * DROWS, 16), DROWS)
                for s in slots:
                    store(s, to, choose(s, lambda i: q_ref[i, rows, :]))

    def store_temporal(s, to, value):
        qall[0, s, to, :] = value

    def store_sliding(s, to, value):
        qslide[s - 2, to, :] = value

    stage_queries(range(2), store_temporal)

    def allowed(half, ids):
        hit = ids == frame * 2 + half
        for n in range(2):
            listed = jnp.where(mask_ref[half, n] == 1, near_ref[half, n], -5)
            hit = hit | (ids == listed)
        return hit

    lane_ids = lax.broadcasted_iota(jnp.int32, (1, HD), 1)
    for s in range(2):
        shift = jnp.where(s < many, 0.0, OFF)
        for half in range(2):
            tsend[s * 2 + half : s * 2 + half + 1, :] = jnp.where(allowed(half, lane_ids), 0.0, shift)
    tsend[4:8, :] = jnp.zeros((4, HD), F32)
    window_ids = frame * 2 - 1 + lax.broadcasted_iota(jnp.int32, (8, HD), 0)
    window = [jnp.where(allowed(half, window_ids), 0.0, OFF) for half in range(2)]

    def query_copy(src, dst, s, g):
        return remote(qall.at[src, s], qall.at[dst, s], q_ss.at[dst, s], q_rs.at[dst, s], at_y(g))

    up = [start(query_copy(0, 3, 0, 1)), None]
    down = [None, start(query_copy(0, 1, 1, 3))]
    up[1] = start(query_copy(0, 3, 1, 1))
    down[0] = start(query_copy(0, 1, 0, 3))
    tx = [None] * 4
    for g in (1, 3, 2):
        tx[g] = start(remote(tsend, trecv.at[4 - g], t_ss.at[g], t_rs.at[4 - g], at_y(g)))

    @pl.loop(0, ROWS // 96)
    def _(r):
        rows = pl.ds(pl.multiple_of(r * 96, 96), 96)
        to = pl.ds(pl.multiple_of(TILE + r * 96, 96), 96)
        for s in range(3):
            for t in range(2):
                wbuf[s, t, to, :] = choose(s + 2, lambda i: kv_ref[t, i, rows, :])

    def spread(src, g):
        for i in range(4):
            row = jnp.broadcast_to(src[i : i + 1, :], (128, 128))
            tab[g, i] = jnp.transpose(row)[0:32]

    spread(tsend[...], 0)
    stage_queries(range(2, 5), store_sliding)

    half_of = [((z + zr) % 4) // 2 for zr in range(4)]

    def rows_bias(get):
        low, high = get(0), get(1)
        blocks = []
        for zr in range(4):
            pick = jnp.where(half_of[zr] == 0, low, high)
            blocks.append(jnp.broadcast_to(pick, (ZROWS, HD)))
        return jnp.concatenate(blocks, axis=0)

    def temporal_bias(g, s, b):
        bias = []
        for d in range(2):
            part = frame_of(xl if b == 0 else 1 - xl, y, c if d == 0 else 1 - c)
            for t in range(2):
                bias.append(rows_bias(lambda half: tab[g, s * 2 + half, pl.ds(part * 2 + t, 1), :]))
        return bias

    def temporal(g, b, chunks, first, done=None):
        items = [(s, k) for s in range(2) for k in chunks]
        bias = [temporal_bias(g, s, b) for s in range(2)]

        def score(item):
            s, k = item
            return scores(qall[g, s, pl.ds(k * CROWS, CROWS), :], kbuf[b, s, 0])

        ahead = score(items[0])
        for i, (s, k) in enumerate(items):
            now = ahead
            if i + 1 < len(items):
                ahead = score(items[i + 1])
            rows = pl.ds(k * CROWS, CROWS)
            if first:
                m, acc = jnp.full((CROWS, HD), NEG, F32), None
            else:
                m, acc = m_ref[g, s, rows, :], acc_ref[g, s, rows, :]
            m, acc = fold(now, kbuf[b, s, 1], bias[s], m, acc)
            m_ref[g, s, rows, :] = m
            acc_ref[g, s, rows, :] = acc
            if done is not None and k == CH - 1:
                done(s)

    def o_copies(g, s):
        return (
            remote(osend.at[g, s], orecv.at[4 - g, s], o_ss.at[g, s], o_rs.at[4 - g, s], at_y(g)),
            remote(lsend.at[g, s], lrecv.at[4 - g, s], l_ss.at[g, s], l_rs.at[4 - g, s], at_y(g)),
        )

    def send_o(g, s):
        total = acc_ref[g, s, :, HD:]
        safe = jnp.where(total > 0, total, 1.0)
        osend[g, s] = (acc_ref[g, s, :, :HD] / safe).astype(BF16)
        log = m_ref[g, s] + jnp.log2(safe)
        lsend[g, s] = jnp.transpose(log)[0:8]
        for copy in o_copies(g, s):
            copy.start()

    for s in range(2):
        kc[0][s].wait_recv()
    temporal(0, 0, range(CH), True)
    up[0].wait_recv()
    far = [start(query_copy(3, 2, 0, 1)), None]
    down[1].wait_recv()
    far[1] = start(query_copy(1, 2, 1, 3))
    down[0].wait_recv()
    up[1].wait_recv()
    for g in (1, 3, 2):
        tx[4 - g].wait_recv()
        spread(trecv[g], g)
    h_next = start(remote(wbuf.at[:, :, pl.ds(2 * TILE, TILE)], wbuf.at[:, :, pl.ds(0, TILE)],
                          h_ss.at[0], h_rs.at[0], after))
    h_prev = start(remote(wbuf.at[:, :, pl.ds(TILE, TILE)], wbuf.at[:, :, pl.ds(3 * TILE, TILE)],
                          h_ss.at[1], h_rs.at[1], before))
    temporal(1, 0, range(CH), True)
    temporal(3, 0, range(CH), True)
    for s in range(2):
        kx[s].wait_recv()
        start(kc[1][s])
    for copy in far:
        copy.wait_recv()
    temporal(2, 0, range(CH), True)
    for s in range(2):
        kc[1][s].wait_recv()

    @pl.loop(0, 2)
    def _(i):
        g = 1 + 2 * i
        temporal(g, 1, range(CH), False)
        for s in range(2):
            send_o(g, s)

    temporal(2, 1, range(CH), False, lambda s: send_o(2, s))
    temporal(0, 1, range(CH), False)

    h_next.wait_recv()
    h_prev.wait_recv()

    window_bias = [
        rows_bias(lambda half, t=t: window[half][t : t + 1, :]) for t in range(4)
    ]
    items = [(s, k) for s in range(3) for k in range(CH)]
    ahead = scores(qslide[0, 0:CROWS, :], wbuf[0, 0])
    for i, (s, k) in enumerate(items):
        now = ahead
        if i + 1 < len(items):
            s1, k1 = items[i + 1]
            ahead = scores(qslide[s1, k1 * CROWS : (k1 + 1) * CROWS, :], wbuf[s1, 0])
        _, acc = fold(now, wbuf[s, 1], window_bias, jnp.full((CROWS, HD), NEG, F32), None)
        attn[k, :, (s + 2) * HD : (s + 3) * HD] = (acc[:, :HD] / acc[:, HD:]).astype(BF16)

    def combine(k):
        rows = pl.ds(k * CROWS, CROWS)
        for s in range(2):
            total = acc_ref[0, s, rows, HD:]
            logs = [m_ref[0, s, rows, :] + jnp.log2(total)]
            outs = [acc_ref[0, s, rows, :HD] / total]
            for g in range(1, 4):
                line = lrecv[g, s, 0:1, k * CROWS : (k + 1) * CROWS]
                logs.append(jnp.transpose(jnp.broadcast_to(line, (HD, CROWS))))
                outs.append(orecv[g, s, rows, :].astype(F32))
            top = functools.reduce(jnp.maximum, logs)
            weights = [jnp.exp2(log - top) for log in logs]
            mixed = functools.reduce(jnp.add, [w * o for w, o in zip(weights, outs)])
            attn[k, :, s * HD : (s + 1) * HD] = (
                mixed / functools.reduce(jnp.add, weights)
            ).astype(BF16)

    WIDTH = 768

    def reorder(k):
        slots = [attn[k, :, s * HD : (s + 1) * HD] for s in range(5)]
        for i in range(5):
            value = slots[0]
            for s in range(1, 5):
                if i in heads_of[s]:
                    value = lax.select(order[s] == i, slots[s], value)
            attn[k, :, i * HD : (i + 1) * HD] = value

    def project(k, first, last):
        whole = (last - first) // WIDTH

        @pl.loop(0, whole)
        def _(j):
            columns = pl.ds(pl.multiple_of(first + j * WIDTH, 128), WIDTH)
            pbuf[k, :, columns] = dot(attn[k], w_ref[:, columns], 1, 0).astype(BF16)

        rest = first + whole * WIDTH
        if rest < last:
            pbuf[k, :, rest:last] = dot(attn[k], w_ref[:, rest:last], 1, 0).astype(BF16)

    def block(k, zr, xr, first, width):
        return pbuf.at[k, pl.ds((zr * 2 + xr) * DROWS, DROWS), pl.ds(first, width)]

    def add(k, zr, xr, first, width, *others):
        @pl.loop(0, DROWS // 16)
        def _(i):
            rows = pl.ds(pl.multiple_of((zr * 2 + xr) * DROWS + i * 16, 16), 16)
            value = pbuf[k, rows, first : first + width].astype(F32)
            for other in others:
                value += other[pl.ds(pl.multiple_of(i * 16, 16), 16), :].astype(F32)
            pbuf[k, rows, first : first + width] = value.astype(BF16)

    def emit(k, first, width, *others):
        @pl.loop(0, DROWS // 16)
        def _(i):
            value = pbuf[k, pl.ds(pl.multiple_of(i * 16, 16), 16), first : first + width].astype(F32)
            for other in others:
                value += other[pl.ds(pl.multiple_of(i * 16, 16), 16), :].astype(F32)
            rows = pl.ds(pl.multiple_of(k * DROWS + i * 16, 16), 16)
            out_ref[rows, first : first + width] = value.astype(BF16)

    H1, H2 = CA, CA + HB

    class Chunk:
        def __init__(self, k):
            self.k = k
            self.count = 0

        def send(self, src, dst, peer):
            n = self.count
            self.count += 1
            return start(remote(src, dst, r_ss.at[self.k, n], r_rs.at[self.k, n], peer))

        def first_a(self):
            k = self.k
            self.fa = [
                self.send(block(k, 2, 0, 0, CA), fa.at[k, 0], z_up),
                self.send(block(k, 2, 1, 0, CA), fa.at[k, 1], z_down),
            ]
            self.ra = [
                self.send(block(k, 1, 1, 0, CA), ra.at[k, 0, 1], z_up),
                self.send(block(k, 3, 0, 0, CA), ra.at[k, 1, 0], z_down),
            ]

        def first_b(self):
            k = self.k
            self.xb = {}
            for zr in (2, 1, 3, 0):
                self.xb[zr] = self.send(block(k, zr, 1, CA, CB), xb.at[k, zr], x_other)

        def forward_a(self):
            k = self.k
            self.fa[0].wait_recv()
            add(k, 1, 0, 0, CA, fa.at[k, 0])
            self.ra.append(self.send(block(k, 1, 0, 0, CA), ra.at[k, 0, 0], z_up))
            self.fa[1].wait_recv()
            add(k, 3, 1, 0, CA, fa.at[k, 1])
            self.ra.append(self.send(block(k, 3, 1, 0, CA), ra.at[k, 1, 1], z_down))

        def second_b(self):
            k = self.k
            self.xb[2].wait_recv()
            add(k, 2, 0, CA, CB, xb.at[k, 2])
            self.fb = [
                self.send(block(k, 2, 0, H1, HB), fb.at[k, 0], z_up),
                self.send(block(k, 2, 0, H2, HB), fb.at[k, 1], z_down),
            ]
            self.xb[1].wait_recv()
            add(k, 1, 0, CA, CB, xb.at[k, 1])
            self.rb = [self.send(block(k, 1, 0, H2, HB), rb.at[k, 0, 1], z_up)]
            self.xb[3].wait_recv()
            add(k, 3, 0, CA, CB, xb.at[k, 3])
            self.rb.append(self.send(block(k, 3, 0, H1, HB), rb.at[k, 1, 0], z_down))

        def third_a(self):
            k = self.k
            for copy in self.ra:
                copy.wait_recv()
            add(k, 0, 1, 0, CA, ra.at[k, 0, 1], ra.at[k, 1, 1])
            self.xa = self.send(block(k, 0, 1, 0, CA), xa.at[k], x_other)

        def forward_b(self):
            k = self.k
            self.fb[0].wait_recv()
            add(k, 1, 0, H1, HB, fb.at[k, 0])
            self.rb.append(self.send(block(k, 1, 0, H1, HB), rb.at[k, 0, 0], z_up))
            self.fb[1].wait_recv()
            add(k, 3, 0, H2, HB, fb.at[k, 1])
            self.rb.append(self.send(block(k, 3, 0, H2, HB), rb.at[k, 1, 1], z_down))

        def finish(self):
            k = self.k
            self.xa.wait_recv()
            emit(k, 0, CA, ra.at[k, 0, 0], ra.at[k, 1, 0], xa.at[k])
            self.xb[0].wait_recv()
            for copy in self.rb:
                copy.wait_recv()
            emit(k, H1, HB, xb.at[k, 0, :, pl.ds(0, HB)], rb.at[k, 0, 0], rb.at[k, 1, 0])
            emit(k, H2, HB, xb.at[k, 0, :, pl.ds(HB, HB)], rb.at[k, 0, 1], rb.at[k, 1, 1])

    one, two = Chunk(0), Chunk(1)
    for g in (1, 3, 2):
        for s in range(2):
            for copy in o_copies(4 - g, s):
                copy.wait_recv()
    combine(0)
    reorder(0)
    load_w.wait()
    project(0, CA, D)
    one.first_b()
    project(0, 0, CA)
    one.first_a()
    combine(1)
    reorder(1)
    project(1, CA, D)
    two.first_b()
    one.forward_a()
    project(1, 0, CA)
    two.first_a()
    one.second_b()
    two.forward_a()
    one.third_a()
    one.forward_b()
    two.second_b()
    two.third_a()
    two.forward_b()
    one.finish()
    two.finish()

    for copy in sent:
        copy.wait_send()
    for g in range(1, 4):
        for s in range(2):
            for copy in o_copies(g, s):
                copy.wait_send()


def per_device(queries, keys_values, head_kind, tile_neighbours, tile_mask, out_weight):
    smem = pl.BlockSpec(memory_space=pltpu.SMEM)
    vmem = pl.BlockSpec(memory_space=pltpu.VMEM)
    dma = pltpu.SemaphoreType.DMA
    return pl.pallas_call(
        kernel,
        out_shape=jax.ShapeDtypeStruct((ROWS // 8, D), BF16),
        in_specs=[
            smem, smem, smem,
            vmem, vmem,
            pl.BlockSpec(memory_space=pl.ANY),
        ],
        out_specs=vmem,
        scratch_shapes=[
            pltpu.VMEM((5 * HD, D), BF16),
            pltpu.VMEM((4, 2, ROWS, HD), BF16),
            pltpu.VMEM((3, ROWS, HD), BF16),
            pltpu.VMEM((2, 2, 2, 2 * ROWS, HD), BF16),
            pltpu.VMEM((3, 2, 4 * TILE, HD), BF16),
            pltpu.VMEM((8, HD), F32),
            pltpu.VMEM((4, 8, HD), F32),
            pltpu.VMEM((4, 4, 32, HD), F32),
            pltpu.VMEM((4, 2, ROWS, HD), F32),
            pltpu.VMEM((4, 2, ROWS, 2 * HD), F32),
            pltpu.VMEM((4, 2, ROWS, HD), BF16),
            pltpu.VMEM((4, 2, 8, ROWS), F32),
            pltpu.VMEM((4, 2, ROWS, HD), BF16),
            pltpu.VMEM((4, 2, 8, ROWS), F32),
            pltpu.VMEM((CH, CROWS, 5 * HD), BF16),
            pltpu.VMEM((CH, CROWS, D), BF16),
            pltpu.VMEM((CH, 2, DROWS, CA), BF16),
            pltpu.VMEM((CH, 2, 2, DROWS, CA), BF16),
            pltpu.VMEM((CH, DROWS, CA), BF16),
            pltpu.VMEM((CH, 4, DROWS, CB), BF16),
            pltpu.VMEM((CH, 2, DROWS, HB), BF16),
            pltpu.VMEM((CH, 2, 2, DROWS, HB), BF16),
            dma,
            dma((4, 2)), dma((4, 2)),
            dma((4,)), dma((4,)),
            dma((2,)), dma((2,)),
            dma((2, 2)), dma((2, 2)),
            dma((2,)), dma((2,)),
            dma((4, 2)), dma((4, 2)),
            dma((4, 2)), dma((4, 2)),
            dma((CH, 20)), dma((CH, 20)),
        ],
        name="attend_project",
        compiler_params=pltpu.CompilerParams(
            collective_id=0, has_side_effects=True, vmem_limit_bytes=60 * 2**20
        ),
    )(
        head_kind,
        tile_neighbours,
        tile_mask,
        jnp.transpose(queries, (1, 0, 2)),
        jnp.transpose(keys_values, (0, 2, 1, 3)),
        out_weight,
    )


def solution(mesh):
    return jax.shard_map(
        per_device,
        mesh=mesh,
        in_specs=(
            P("frame", "head", None),
            P(None, "frame", "head", None),
            P("head"),
            P("frame", None),
            P("frame", None),
            P("head", None),
        ),
        out_specs=P(("frame", "head"), None),
        check_vma=False,
    )
```

```python
import functools
import math

import jax
import jax.numpy as jnp
from jax import lax
from jax.experimental import pallas as pl
from jax.experimental.pallas import tpu as pltpu
from jax.sharding import PartitionSpec as P

MESH = pl.DeviceIdType.MESH
F32 = jnp.float32
BF16 = jnp.bfloat16

ROWS = 768
TILE = 384
HD = 128
D = 5120
CH = 2
CROWS = ROWS // CH
DROWS = CROWS // 8
ZROWS = 2 * DROWS
CA = 1536
CB = 1536
CE = D - CA - CB
EW = CA + CB
HB, HE = CB // 2, CE // 2
WROWS = 5 * HD // 2
NEG = -1e30
OFF = -2e30
SCALE = HD**-0.5 * math.log2(math.e)


def dot(a, b, ca, cb):
    return lax.dot_general(a, b, (((ca,), (cb,)), ((), ())), preferred_element_type=F32)


def scores(q, k):
    scaled = q.astype(F32) * SCALE
    high = scaled.astype(BF16)
    low = (scaled - high.astype(F32)).astype(BF16)
    return dot(jnp.concatenate([high, low], axis=1), jnp.concatenate([k, k], axis=1), 1, 1)


def fold(s, v, bias, m, acc):
    tiles = len(bias)
    rows = s.shape[0]
    new = m
    for t in range(tiles):
        part = s[:, t * TILE : (t + 1) * TILE]
        top = jnp.broadcast_to(jnp.max(part, axis=1, keepdims=True), (rows, HD))
        new = jnp.maximum(new, top + bias[t])
    pieces = []
    for t in range(tiles):
        sub = new - bias[t]
        for u in range(TILE // HD):
            at = t * TILE + u * HD
            pieces.append(jnp.exp2(s[:, at : at + HD] - sub).astype(BF16))
    o = dot(jnp.concatenate(pieces, axis=1), jnp.concatenate([v, jnp.ones_like(v)], axis=1), 1, 0)
    if acc is None:
        return new, o
    f = jnp.exp2(m - new)
    return new, acc * jnp.concatenate([f, f], axis=1) + o


def kernel(
    kind_ref, near_ref, mask_ref, q_ref, kv_ref, w_hbm, out_ref,
    w_ref, qall, qslide, kbuf, wbuf, tsend, trecv, tab, m_ref, acc_ref,
    osend, lsend, orecv, lrecv, attn, pbuf,
    fa, ra, xa, xb, fb, rb, wx, asend, arecv, fe, re,
    w_sem, q_ss, q_rs, t_ss, t_rs, kx_ss, kx_rs, kc_ss, kc_rs, h_ss, h_rs,
    o_ss, o_rs, l_ss, l_rs, r_ss, r_rs, wx_ss, wx_rs, a_ss, a_rs,
):
    frame = lax.axis_index("frame")
    head = lax.axis_index("head")
    xl, y, c = frame // 8, (frame // 2) % 4, frame % 2
    z, xh = head // 2, head % 2

    def frame_of(a, b, d):
        return (a * 4 + b) * 2 + d

    def at_y(g):
        return (frame_of(xl, (y + g) % 4, c), head)

    core = (frame_of(xl, y, 1 - c), head)
    across = (frame_of(1 - xl, y, c), head)
    after = ((frame + 1) % 16, head)
    before = ((frame + 15) % 16, head)
    z_up = (frame, ((z + 1) % 4) * 2 + xh)
    z_down = (frame, ((z + 3) % 4) * 2 + xh)
    x_other = (frame, z * 2 + 1 - xh)

    load_w = pltpu.make_async_copy(w_hbm, w_ref, w_sem)
    load_w.start()

    barrier = pltpu.get_barrier_semaphore()
    peers = [at_y(1), at_y(2), at_y(3), core, across, after, before, z_up, z_down, x_other]
    for peer in peers:
        pl.semaphore_signal(barrier, inc=1, device_id=peer, device_id_type=MESH)
    pl.semaphore_wait(barrier, len(peers))

    def remote(src, dst, ss, rs, peer):
        return pltpu.make_async_remote_copy(
            src_ref=src, dst_ref=dst, send_sem=ss, recv_sem=rs, device_id=peer, device_id_type=MESH
        )

    sent = []

    def start(copy):
        copy.start()
        sent.append(copy)
        return copy

    kinds = [kind_ref[i] for i in range(5)]
    many = functools.reduce(jnp.add, kinds)
    order = [0] * 5
    seen = 0
    for i in range(5):
        slot = jnp.where(kinds[i] == 1, seen, many + i - seen)
        seen = seen + kinds[i]
        order = [jnp.where(slot == s, i, order[s]) for s in range(5)]
    heads_of = [range(5), range(5), range(0, 3), range(1, 4), range(2, 5)]

    def choose(s, get):
        value = get(heads_of[s][0])
        for i in heads_of[s][1:]:
            value = lax.select(order[s] == i, get(i), value)
        return value

    @pl.loop(0, ROWS // 96)
    def _(r):
        rows = pl.ds(pl.multiple_of(r * 96, 96), 96)
        for s in range(2):
            for t in range(2):
                kbuf[0, s, t, rows, :] = choose(s, lambda i: kv_ref[t, i, rows, :])

    kx = [
        start(remote(kbuf.at[0, s, :, pl.ds(0, ROWS)], kbuf.at[1, s, :, pl.ds(0, ROWS)],
                     kx_ss.at[s], kx_rs.at[s], across))
        for s in range(2)
    ]
    kc = [
        [remote(kbuf.at[b, s, :, pl.ds(0, ROWS)], kbuf.at[b, s, :, pl.ds(ROWS, ROWS)],
                kc_ss.at[b, s], kc_rs.at[b, s], core) for s in range(2)]
        for b in range(2)
    ]
    for s in range(2):
        start(kc[0][s])
    def stage_queries(slots, store):
        for k in range(CH):

            @pl.loop(0, 8)
            def _(d):
                dest = ((z + d // 2) % 4) * 2 + (xh + d % 2) % 2
                rows = pl.ds(pl.multiple_of((dest * CH + k) * DROWS, 16), DROWS)
                to = pl.ds(pl.multiple_of(k * CROWS + d * DROWS, 16), DROWS)
                for s in slots:
                    store(s, to, choose(s, lambda i: q_ref[i, rows, :]))

    def store_temporal(s, to, value):
        qall[0, s, to, :] = value

    def store_sliding(s, to, value):
        qslide[s - 2, to, :] = value

    stage_queries(range(2), store_temporal)

    def allowed(half, ids):
        hit = ids == frame * 2 + half
        for n in range(2):
            listed = jnp.where(mask_ref[half, n] == 1, near_ref[half, n], -5)
            hit = hit | (ids == listed)
        return hit

    lane_ids = lax.broadcasted_iota(jnp.int32, (1, HD), 1)
    for s in range(2):
        shift = jnp.where(s < many, 0.0, OFF)
        for half in range(2):
            tsend[s * 2 + half : s * 2 + half + 1, :] = jnp.where(allowed(half, lane_ids), 0.0, shift)
    tsend[4:8, :] = jnp.zeros((4, HD), F32)
    window_ids = frame * 2 - 1 + lax.broadcasted_iota(jnp.int32, (8, HD), 0)
    window = [jnp.where(allowed(half, window_ids), 0.0, OFF) for half in range(2)]

    def query_copy(src, dst, s, g):
        return remote(qall.at[src, s], qall.at[dst, s], q_ss.at[dst, s], q_rs.at[dst, s], at_y(g))

    up = [start(query_copy(0, 3, 0, 1)), None]
    down = [None, start(query_copy(0, 1, 1, 3))]
    up[1] = start(query_copy(0, 3, 1, 1))
    down[0] = start(query_copy(0, 1, 0, 3))
    tx = [None] * 4
    for g in (1, 3, 2):
        tx[g] = start(remote(tsend, trecv.at[4 - g], t_ss.at[g], t_rs.at[4 - g], at_y(g)))

    @pl.loop(0, ROWS // 96)
    def _(r):
        rows = pl.ds(pl.multiple_of(r * 96, 96), 96)
        to = pl.ds(pl.multiple_of(TILE + r * 96, 96), 96)
        for s in range(3):
            for t in range(2):
                wbuf[s, t, to, :] = choose(s + 2, lambda i: kv_ref[t, i, rows, :])

    def spread(src, g):
        for i in range(4):
            row = jnp.broadcast_to(src[i : i + 1, :], (128, 128))
            tab[g, i] = jnp.transpose(row)[0:32]

    spread(tsend[...], 0)
    stage_queries(range(2, 5), store_sliding)

    half_of = [((z + zr) % 4) // 2 for zr in range(4)]

    def rows_bias(get):
        low, high = get(0), get(1)
        blocks = []
        for zr in range(4):
            pick = jnp.where(half_of[zr] == 0, low, high)
            blocks.append(jnp.broadcast_to(pick, (ZROWS, HD)))
        return jnp.concatenate(blocks, axis=0)

    def temporal_bias(g, s, b):
        bias = []
        for d in range(2):
            part = frame_of(xl if b == 0 else 1 - xl, y, c if d == 0 else 1 - c)
            for t in range(2):
                bias.append(rows_bias(lambda half: tab[g, s * 2 + half, pl.ds(part * 2 + t, 1), :]))
        return bias

    def temporal(g, b, chunks, first, done=None):
        items = [(s, k) for s in range(2) for k in chunks]
        bias = [temporal_bias(g, s, b) for s in range(2)]

        def score(item):
            s, k = item
            return scores(qall[g, s, pl.ds(k * CROWS, CROWS), :], kbuf[b, s, 0])

        ahead = score(items[0])
        for i, (s, k) in enumerate(items):
            now = ahead
            if i + 1 < len(items):
                ahead = score(items[i + 1])
            rows = pl.ds(k * CROWS, CROWS)
            if first:
                m, acc = jnp.full((CROWS, HD), NEG, F32), None
            else:
                m, acc = m_ref[g, s, rows, :], acc_ref[g, s, rows, :]
            m, acc = fold(now, kbuf[b, s, 1], bias[s], m, acc)
            m_ref[g, s, rows, :] = m
            acc_ref[g, s, rows, :] = acc
            if done is not None and k == CH - 1:
                done(s)

    def o_copies(g, s):
        return (
            remote(osend.at[g, s], orecv.at[4 - g, s], o_ss.at[g, s], o_rs.at[4 - g, s], at_y(g)),
            remote(lsend.at[g, s], lrecv.at[4 - g, s], l_ss.at[g, s], l_rs.at[4 - g, s], at_y(g)),
        )

    def send_o(g, s):
        total = acc_ref[g, s, :, HD:]
        safe = jnp.where(total > 0, total, 1.0)
        osend[g, s] = (acc_ref[g, s, :, :HD] / safe).astype(BF16)
        log = m_ref[g, s] + jnp.log2(safe)
        lsend[g, s] = jnp.transpose(log)[0:8]
        for copy in o_copies(g, s):
            copy.start()

    for s in range(2):
        kc[0][s].wait_recv()
    temporal(0, 0, range(CH), True)
    up[0].wait_recv()
    far = [start(query_copy(3, 2, 0, 1)), None]
    down[1].wait_recv()
    far[1] = start(query_copy(1, 2, 1, 3))
    down[0].wait_recv()
    up[1].wait_recv()
    for g in (1, 3, 2):
        tx[4 - g].wait_recv()
        spread(trecv[g], g)
    h_next = start(remote(wbuf.at[:, :, pl.ds(2 * TILE, TILE)], wbuf.at[:, :, pl.ds(0, TILE)],
                          h_ss.at[0], h_rs.at[0], after))
    h_prev = start(remote(wbuf.at[:, :, pl.ds(TILE, TILE)], wbuf.at[:, :, pl.ds(3 * TILE, TILE)],
                          h_ss.at[1], h_rs.at[1], before))
    temporal(1, 0, range(CH), True)
    temporal(3, 0, range(CH), True)
    for s in range(2):
        kx[s].wait_recv()
        start(kc[1][s])
    load_w.wait()
    mine = pl.ds(pl.multiple_of(c * WROWS, 16), WROWS)
    w_cross = start(remote(w_ref.at[mine, pl.ds(EW, CE)], wx.at[mine], wx_ss.at[0], wx_rs.at[0], x_other))
    w_core = remote(wx.at[mine], wx.at[mine], wx_ss.at[1], wx_rs.at[1], core)
    for copy in far:
        copy.wait_recv()
    temporal(2, 0, range(CH), True)
    for s in range(2):
        kc[1][s].wait_recv()

    @pl.loop(0, 2)
    def _(i):
        g = 1 + 2 * i
        temporal(g, 1, range(CH), False)
        for s in range(2):
            send_o(g, s)

    temporal(2, 1, range(CH), False, lambda s: send_o(2, s))
    temporal(0, 1, range(CH), False)

    h_next.wait_recv()
    h_prev.wait_recv()

    window_bias = [
        rows_bias(lambda half, t=t: window[half][t : t + 1, :]) for t in range(4)
    ]
    items = [(s, k) for s in range(3) for k in range(CH)]
    ahead = scores(qslide[0, 0:CROWS, :], wbuf[0, 0])
    for i, (s, k) in enumerate(items):
        now = ahead
        if i + 1 < len(items):
            s1, k1 = items[i + 1]
            ahead = scores(qslide[s1, k1 * CROWS : (k1 + 1) * CROWS, :], wbuf[s1, 0])
        _, acc = fold(now, wbuf[s, 1], window_bias, jnp.full((CROWS, HD), NEG, F32), None)
        attn[k, :, (s + 2) * HD : (s + 3) * HD] = (acc[:, :HD] / acc[:, HD:]).astype(BF16)

    def combine(k):
        rows = pl.ds(k * CROWS, CROWS)
        for s in range(2):
            total = acc_ref[0, s, rows, HD:]
            logs = [m_ref[0, s, rows, :] + jnp.log2(total)]
            outs = [acc_ref[0, s, rows, :HD] / total]
            for g in range(1, 4):
                line = lrecv[g, s, 0:1, k * CROWS : (k + 1) * CROWS]
                logs.append(jnp.transpose(jnp.broadcast_to(line, (HD, CROWS))))
                outs.append(orecv[g, s, rows, :].astype(F32))
            top = functools.reduce(jnp.maximum, logs)
            weights = [jnp.exp2(log - top) for log in logs]
            mixed = functools.reduce(jnp.add, [w * o for w, o in zip(weights, outs)])
            attn[k, :, s * HD : (s + 1) * HD] = (
                mixed / functools.reduce(jnp.add, weights)
            ).astype(BF16)

    WIDTH = 768

    def reorder(k):
        slots = [attn[k, :, s * HD : (s + 1) * HD] for s in range(5)]
        for i in range(5):
            value = slots[0]
            for s in range(1, 5):
                if i in heads_of[s]:
                    value = lax.select(order[s] == i, slots[s], value)
            attn[k, :, i * HD : (i + 1) * HD] = value

    def project(k, first, last):
        whole = (last - first) // WIDTH

        @pl.loop(0, whole)
        def _(j):
            columns = pl.ds(pl.multiple_of(first + j * WIDTH, 128), WIDTH)
            pbuf[k, :, columns] = dot(attn[k], w_ref[:, columns], 1, 0).astype(BF16)

        rest = first + whole * WIDTH
        if rest < last:
            pbuf[k, :, rest:last] = dot(attn[k], w_ref[:, rest:last], 1, 0).astype(BF16)

    def exchange(k):
        for zr in range(4):
            at = (zr * 2 + 1) * DROWS
            asend[k, zr * DROWS : (zr + 1) * DROWS, :] = attn[k, at : at + DROWS, :]
        return start(remote(asend.at[k], arecv.at[k], a_ss.at[k], a_rs.at[k], x_other))

    def project_two(k):
        kept = jnp.concatenate(
            [attn[k, zr * ZROWS : zr * ZROWS + DROWS, :] for zr in range(4)], axis=0
        )

        @pl.loop(0, CE // 512)
        def _(j):
            columns = pl.ds(pl.multiple_of(EW + j * 512, 512), 512)
            others = pl.ds(pl.multiple_of(j * 512, 512), 512)
            value = dot(kept, w_ref[:, columns], 1, 0) + dot(arecv[k], wx[:, others], 1, 0)
            value = value.astype(BF16)
            for zr in range(4):
                pbuf[k, zr * ZROWS : zr * ZROWS + DROWS, columns] = value[zr * DROWS : (zr + 1) * DROWS]

    def block(k, zr, xr, first, width):
        return pbuf.at[k, pl.ds((zr * 2 + xr) * DROWS, DROWS), pl.ds(first, width)]

    def add(k, zr, xr, first, width, *others):
        @pl.loop(0, DROWS // 16)
        def _(i):
            rows = pl.ds(pl.multiple_of((zr * 2 + xr) * DROWS + i * 16, 16), 16)
            value = pbuf[k, rows, first : first + width].astype(F32)
            for other in others:
                value += other[pl.ds(pl.multiple_of(i * 16, 16), 16), :].astype(F32)
            pbuf[k, rows, first : first + width] = value.astype(BF16)

    def emit(k, first, width, *others):
        @pl.loop(0, DROWS // 16)
        def _(i):
            value = pbuf[k, pl.ds(pl.multiple_of(i * 16, 16), 16), first : first + width].astype(F32)
            for other in others:
                value += other[pl.ds(pl.multiple_of(i * 16, 16), 16), :].astype(F32)
            rows = pl.ds(pl.multiple_of(k * DROWS + i * 16, 16), 16)
            out_ref[rows, first : first + width] = value.astype(BF16)

    H1, H2 = CA, CA + HB

    class Chunk:
        def __init__(self, k):
            self.k = k
            self.count = 0

        def send(self, src, dst, peer):
            n = self.count
            self.count += 1
            return start(remote(src, dst, r_ss.at[self.k, n], r_rs.at[self.k, n], peer))

        def first_a(self):
            k = self.k
            self.fa = [
                self.send(block(k, 2, 0, 0, CA), fa.at[k, 0], z_up),
                self.send(block(k, 2, 1, 0, CA), fa.at[k, 1], z_down),
            ]
            self.ra = [
                self.send(block(k, 1, 1, 0, CA), ra.at[k, 0, 1], z_up),
                self.send(block(k, 3, 0, 0, CA), ra.at[k, 1, 0], z_down),
            ]

        def first_b(self):
            k = self.k
            self.xb = {}
            for zr in (2, 1, 3, 0):
                self.xb[zr] = self.send(block(k, zr, 1, CA, CB), xb.at[k, zr], x_other)

        def forward_a(self):
            k = self.k
            self.fa[0].wait_recv()
            add(k, 1, 0, 0, CA, fa.at[k, 0])
            self.ra.append(self.send(block(k, 1, 0, 0, CA), ra.at[k, 0, 0], z_up))
            self.fa[1].wait_recv()
            add(k, 3, 1, 0, CA, fa.at[k, 1])
            self.ra.append(self.send(block(k, 3, 1, 0, CA), ra.at[k, 1, 1], z_down))

        def second_b(self):
            k = self.k
            self.xb[2].wait_recv()
            add(k, 2, 0, CA, CB, xb.at[k, 2])
            self.fb = [
                self.send(block(k, 2, 0, H1, HB), fb.at[k, 0], z_up),
                self.send(block(k, 2, 0, H2, HB), fb.at[k, 1], z_down),
            ]
            self.xb[1].wait_recv()
            add(k, 1, 0, CA, CB, xb.at[k, 1])
            self.rb = [self.send(block(k, 1, 0, H2, HB), rb.at[k, 0, 1], z_up)]
            self.xb[3].wait_recv()
            add(k, 3, 0, CA, CB, xb.at[k, 3])
            self.rb.append(self.send(block(k, 3, 0, H1, HB), rb.at[k, 1, 0], z_down))

        def first_e(self):
            k = self.k
            self.fe = [
                self.send(block(k, 2, 0, EW, HE), fe.at[k, 0], z_up),
                self.send(block(k, 2, 0, EW + HE, HE), fe.at[k, 1], z_down),
            ]
            self.re = [
                self.send(block(k, 1, 0, EW + HE, HE), re.at[k, 0, 1], z_up),
                self.send(block(k, 3, 0, EW, HE), re.at[k, 1, 0], z_down),
            ]

        def forward_e(self):
            k = self.k
            self.fe[0].wait_recv()
            add(k, 1, 0, EW, HE, fe.at[k, 0])
            self.re.append(self.send(block(k, 1, 0, EW, HE), re.at[k, 0, 0], z_up))
            self.fe[1].wait_recv()
            add(k, 3, 0, EW + HE, HE, fe.at[k, 1])
            self.re.append(self.send(block(k, 3, 0, EW + HE, HE), re.at[k, 1, 1], z_down))

        def finish_e(self):
            k = self.k
            for copy in self.re:
                copy.wait_recv()
            emit(k, EW, HE, re.at[k, 0, 0], re.at[k, 1, 0])
            emit(k, EW + HE, HE, re.at[k, 0, 1], re.at[k, 1, 1])

        def third_a(self):
            k = self.k
            for copy in self.ra:
                copy.wait_recv()
            add(k, 0, 1, 0, CA, ra.at[k, 0, 1], ra.at[k, 1, 1])
            self.xa = self.send(block(k, 0, 1, 0, CA), xa.at[k], x_other)

        def forward_b(self):
            k = self.k
            self.fb[0].wait_recv()
            add(k, 1, 0, H1, HB, fb.at[k, 0])
            self.rb.append(self.send(block(k, 1, 0, H1, HB), rb.at[k, 0, 0], z_up))
            self.fb[1].wait_recv()
            add(k, 3, 0, H2, HB, fb.at[k, 1])
            self.rb.append(self.send(block(k, 3, 0, H2, HB), rb.at[k, 1, 1], z_down))

        def finish(self):
            k = self.k
            self.xa.wait_recv()
            emit(k, 0, CA, ra.at[k, 0, 0], ra.at[k, 1, 0], xa.at[k])
            self.xb[0].wait_recv()
            for copy in self.rb:
                copy.wait_recv()
            emit(k, H1, HB, xb.at[k, 0, :, pl.ds(0, HB)], rb.at[k, 0, 0], rb.at[k, 1, 0])
            emit(k, H2, HB, xb.at[k, 0, :, pl.ds(HB, HB)], rb.at[k, 0, 1], rb.at[k, 1, 1])

    one, two = Chunk(0), Chunk(1)
    for g in (1, 3, 2):
        for s in range(2):
            for copy in o_copies(4 - g, s):
                copy.wait_recv()
    combine(0)
    reorder(0)
    crossed = [exchange(0)]
    project(0, CA, EW)
    one.first_b()
    project(0, 0, CA)
    one.first_a()
    w_cross.wait_recv()
    start(w_core)
    combine(1)
    reorder(1)
    crossed.append(exchange(1))
    project(1, CA, EW)
    two.first_b()
    project(1, 0, CA)
    two.first_a()
    w_core.wait_recv()
    crossed[0].wait_recv()
    project_two(0)
    one.first_e()
    one.forward_a()
    crossed[1].wait_recv()
    project_two(1)
    two.first_e()
    two.forward_a()
    one.forward_e()
    one.second_b()
    one.third_a()
    two.forward_e()
    one.forward_b()
    two.second_b()
    two.third_a()
    two.forward_b()
    one.finish_e()
    two.finish_e()
    one.finish()
    two.finish()

    for copy in sent:
        copy.wait_send()
    for g in range(1, 4):
        for s in range(2):
            for copy in o_copies(g, s):
                copy.wait_send()


def per_device(queries, keys_values, head_kind, tile_neighbours, tile_mask, out_weight):
    smem = pl.BlockSpec(memory_space=pltpu.SMEM)
    vmem = pl.BlockSpec(memory_space=pltpu.VMEM)
    dma = pltpu.SemaphoreType.DMA
    return pl.pallas_call(
        kernel,
        out_shape=jax.ShapeDtypeStruct((ROWS // 8, D), BF16),
        in_specs=[
            smem, smem, smem,
            vmem, vmem,
            pl.BlockSpec(memory_space=pl.ANY),
        ],
        out_specs=vmem,
        scratch_shapes=[
            pltpu.VMEM((5 * HD, D), BF16),
            pltpu.VMEM((4, 2, ROWS, HD), BF16),
            pltpu.VMEM((3, ROWS, HD), BF16),
            pltpu.VMEM((2, 2, 2, 2 * ROWS, HD), BF16),
            pltpu.VMEM((3, 2, 4 * TILE, HD), BF16),
            pltpu.VMEM((8, HD), F32),
            pltpu.VMEM((4, 8, HD), F32),
            pltpu.VMEM((4, 4, 32, HD), F32),
            pltpu.VMEM((4, 2, ROWS, HD), F32),
            pltpu.VMEM((4, 2, ROWS, 2 * HD), F32),
            pltpu.VMEM((4, 2, ROWS, HD), BF16),
            pltpu.VMEM((4, 2, 8, ROWS), F32),
            pltpu.VMEM((4, 2, ROWS, HD), BF16),
            pltpu.VMEM((4, 2, 8, ROWS), F32),
            pltpu.VMEM((CH, CROWS, 5 * HD), BF16),
            pltpu.VMEM((CH, CROWS, D), BF16),
            pltpu.VMEM((CH, 2, DROWS, CA), BF16),
            pltpu.VMEM((CH, 2, 2, DROWS, CA), BF16),
            pltpu.VMEM((CH, DROWS, CA), BF16),
            pltpu.VMEM((CH, 4, DROWS, CB), BF16),
            pltpu.VMEM((CH, 2, DROWS, HB), BF16),
            pltpu.VMEM((CH, 2, 2, DROWS, HB), BF16),
            pltpu.VMEM((5 * HD, CE), BF16),
            pltpu.VMEM((CH, CROWS // 2, 5 * HD), BF16),
            pltpu.VMEM((CH, CROWS // 2, 5 * HD), BF16),
            pltpu.VMEM((CH, 2, DROWS, HE), BF16),
            pltpu.VMEM((CH, 2, 2, DROWS, HE), BF16),
            dma,
            dma((4, 2)), dma((4, 2)),
            dma((4,)), dma((4,)),
            dma((2,)), dma((2,)),
            dma((2, 2)), dma((2, 2)),
            dma((2,)), dma((2,)),
            dma((4, 2)), dma((4, 2)),
            dma((4, 2)), dma((4, 2)),
            dma((CH, 30)), dma((CH, 30)),
            dma((2,)), dma((2,)),
            dma((CH,)), dma((CH,)),
        ],
        name="attend_project",
        compiler_params=pltpu.CompilerParams(
            collective_id=0, has_side_effects=True, vmem_limit_bytes=60 * 2**20
        ),
    )(
        head_kind,
        tile_neighbours,
        tile_mask,
        jnp.transpose(queries, (1, 0, 2)),
        jnp.transpose(keys_values, (0, 2, 1, 3)),
        out_weight,
    )


def solution(mesh):
    return jax.shard_map(
        per_device,
        mesh=mesh,
        in_specs=(
            P("frame", "head", None),
            P(None, "frame", "head", None),
            P("head"),
            P("frame", None),
            P("frame", None),
            P("head", None),
        ),
        out_specs=P(("frame", "head"), None),
        check_vma=False,
    )
```

```python
import functools
import math

import jax
import jax.numpy as jnp
from jax import lax
from jax.experimental import pallas as pl
from jax.experimental.pallas import tpu as pltpu
from jax.sharding import PartitionSpec as P

MESH = pl.DeviceIdType.MESH
F32 = jnp.float32
BF16 = jnp.bfloat16

ROWS = 768
TILE = 384
HD = 128
D = 5120
CH = 2
CROWS = ROWS // CH
DROWS = CROWS // 8
ZROWS = 2 * DROWS
CA = 1792
CB = 1280
CE = D - CA - CB
EW = CA + CB
HB, HE = CB // 2, CE // 2
WROWS = 5 * HD // 2
NEG = -1e30
OFF = -2e30
SCALE = HD**-0.5 * math.log2(math.e)


def dot(a, b, ca, cb):
    return lax.dot_general(a, b, (((ca,), (cb,)), ((), ())), preferred_element_type=F32)


def scores(q, k):
    scaled = q.astype(F32) * SCALE
    high = scaled.astype(BF16)
    low = (scaled - high.astype(F32)).astype(BF16)
    return dot(jnp.concatenate([high, low], axis=1), jnp.concatenate([k, k], axis=1), 1, 1)


def fold(s, v, bias, m, acc):
    tiles = len(bias)
    rows = s.shape[0]
    new = m
    for t in range(tiles):
        part = s[:, t * TILE : (t + 1) * TILE]
        top = jnp.broadcast_to(jnp.max(part, axis=1, keepdims=True), (rows, HD))
        new = jnp.maximum(new, top + bias[t])
    pieces = []
    for t in range(tiles):
        sub = new - bias[t]
        for u in range(TILE // HD):
            at = t * TILE + u * HD
            pieces.append(jnp.exp2(s[:, at : at + HD] - sub).astype(BF16))
    o = dot(jnp.concatenate(pieces, axis=1), jnp.concatenate([v, jnp.ones_like(v)], axis=1), 1, 0)
    if acc is None:
        return new, o
    f = jnp.exp2(m - new)
    return new, acc * jnp.concatenate([f, f], axis=1) + o


def kernel(
    kind_ref, near_ref, mask_ref, q_ref, kv_ref, w_hbm, out_ref,
    w_ref, qall, qslide, kbuf, wbuf, tsend, trecv, tab, m_ref, acc_ref,
    osend, lsend, orecv, lrecv, attn, pbuf,
    fa, ra, xa, xb, fb, rb, wx, asend, arecv, fe, re,
    w_sem, q_ss, q_rs, t_ss, t_rs, kx_ss, kx_rs, kc_ss, kc_rs, h_ss, h_rs,
    o_ss, o_rs, l_ss, l_rs, r_ss, r_rs, wx_ss, wx_rs, a_ss, a_rs,
):
    frame = lax.axis_index("frame")
    head = lax.axis_index("head")
    xl, y, c = frame // 8, (frame // 2) % 4, frame % 2
    z, xh = head // 2, head % 2

    def frame_of(a, b, d):
        return (a * 4 + b) * 2 + d

    def at_y(g):
        return (frame_of(xl, (y + g) % 4, c), head)

    core = (frame_of(xl, y, 1 - c), head)
    across = (frame_of(1 - xl, y, c), head)
    after = ((frame + 1) % 16, head)
    before = ((frame + 15) % 16, head)
    z_up = (frame, ((z + 1) % 4) * 2 + xh)
    z_down = (frame, ((z + 3) % 4) * 2 + xh)
    x_other = (frame, z * 2 + 1 - xh)

    load_w = pltpu.make_async_copy(w_hbm, w_ref, w_sem)
    load_w.start()

    barrier = pltpu.get_barrier_semaphore()
    peers = [at_y(1), at_y(2), at_y(3), core, across, after, before, z_up, z_down, x_other]
    for peer in peers:
        pl.semaphore_signal(barrier, inc=1, device_id=peer, device_id_type=MESH)
    pl.semaphore_wait(barrier, len(peers))

    def remote(src, dst, ss, rs, peer):
        return pltpu.make_async_remote_copy(
            src_ref=src, dst_ref=dst, send_sem=ss, recv_sem=rs, device_id=peer, device_id_type=MESH
        )

    sent = []

    def start(copy):
        copy.start()
        sent.append(copy)
        return copy

    kinds = [kind_ref[i] for i in range(5)]
    many = functools.reduce(jnp.add, kinds)
    order = [0] * 5
    seen = 0
    for i in range(5):
        slot = jnp.where(kinds[i] == 1, seen, many + i - seen)
        seen = seen + kinds[i]
        order = [jnp.where(slot == s, i, order[s]) for s in range(5)]
    heads_of = [range(5), range(5), range(0, 3), range(1, 4), range(2, 5)]

    def choose(s, get):
        value = get(heads_of[s][0])
        for i in heads_of[s][1:]:
            value = lax.select(order[s] == i, get(i), value)
        return value

    @pl.loop(0, ROWS // 96)
    def _(r):
        rows = pl.ds(pl.multiple_of(r * 96, 96), 96)
        for s in range(2):
            for t in range(2):
                kbuf[0, s, t, rows, :] = choose(s, lambda i: kv_ref[t, i, rows, :])

    kx = [
        remote(kbuf.at[0, s, :, pl.ds(0, ROWS)], kbuf.at[1, s, :, pl.ds(0, ROWS)],
               kx_ss.at[s], kx_rs.at[s], across)
        for s in range(2)
    ]
    kx[0].start()
    kc = [
        [remote(kbuf.at[b, s, :, pl.ds(0, ROWS)], kbuf.at[b, s, :, pl.ds(ROWS, ROWS)],
                kc_ss.at[b, s], kc_rs.at[b, s], core) for s in range(2)]
        for b in range(2)
    ]
    for s in range(2):
        start(kc[0][s])
    def stage_queries(slots, store):
        for k in range(CH):

            @pl.loop(0, 8)
            def _(d):
                dest = ((z + d // 2) % 4) * 2 + (xh + d % 2) % 2
                rows = pl.ds(pl.multiple_of((dest * CH + k) * DROWS, 16), DROWS)
                to = pl.ds(pl.multiple_of(k * CROWS + d * DROWS, 16), DROWS)
                for s in slots:
                    store(s, to, choose(s, lambda i: q_ref[i, rows, :]))

    def store_temporal(s, to, value):
        qall[0, s, to, :] = value

    def store_sliding(s, to, value):
        qslide[s - 2, to, :] = value

    stage_queries(range(2), store_temporal)

    def allowed(half, ids):
        hit = ids == frame * 2 + half
        for n in range(2):
            listed = jnp.where(mask_ref[half, n] == 1, near_ref[half, n], -5)
            hit = hit | (ids == listed)
        return hit

    lane_ids = lax.broadcasted_iota(jnp.int32, (1, HD), 1)
    for s in range(2):
        shift = jnp.where(s < many, 0.0, OFF)
        for half in range(2):
            tsend[s * 2 + half : s * 2 + half + 1, :] = jnp.where(allowed(half, lane_ids), 0.0, shift)
    tsend[4:8, :] = jnp.zeros((4, HD), F32)
    window_ids = frame * 2 - 1 + lax.broadcasted_iota(jnp.int32, (8, HD), 0)
    window = [jnp.where(allowed(half, window_ids), 0.0, OFF) for half in range(2)]

    def query_copy(src, dst, s, g):
        return remote(qall.at[src, s], qall.at[dst, s], q_ss.at[dst, s], q_rs.at[dst, s], at_y(g))

    up = [start(query_copy(0, 3, 0, 1)), None]
    down = [None, start(query_copy(0, 1, 1, 3))]
    up[1] = start(query_copy(0, 3, 1, 1))
    down[0] = start(query_copy(0, 1, 0, 3))
    tx = [None] * 4
    for g in (1, 3, 2):
        tx[g] = start(remote(tsend, trecv.at[4 - g], t_ss.at[g], t_rs.at[4 - g], at_y(g)))

    @pl.loop(0, ROWS // 96)
    def _(r):
        rows = pl.ds(pl.multiple_of(r * 96, 96), 96)
        to = pl.ds(pl.multiple_of(TILE + r * 96, 96), 96)
        for s in range(3):
            for t in range(2):
                wbuf[s, t, to, :] = choose(s + 2, lambda i: kv_ref[t, i, rows, :])

    def spread(src, g):
        for i in range(4):
            row = jnp.broadcast_to(src[i : i + 1, :], (128, 128))
            tab[g, i] = jnp.transpose(row)[0:32]

    spread(tsend[...], 0)
    stage_queries(range(2, 5), store_sliding)

    half_of = [((z + zr) % 4) // 2 for zr in range(4)]

    def rows_bias(get):
        low, high = get(0), get(1)
        blocks = []
        for zr in range(4):
            pick = jnp.where(half_of[zr] == 0, low, high)
            blocks.append(jnp.broadcast_to(pick, (ZROWS, HD)))
        return jnp.concatenate(blocks, axis=0)

    def temporal_bias(g, s, b):
        bias = []
        for d in range(2):
            part = frame_of(xl if b == 0 else 1 - xl, y, c if d == 0 else 1 - c)
            for t in range(2):
                bias.append(rows_bias(lambda half: tab[g, s * 2 + half, pl.ds(part * 2 + t, 1), :]))
        return bias

    def temporal(groups, first, done=None):
        items = [(g, b, s, k) for g, b, s in groups for k in range(CH)]
        bias = {group: temporal_bias(group[0], group[2], group[1]) for group in groups}

        def score(item):
            g, b, s, k = item
            return scores(qall[g, s, pl.ds(k * CROWS, CROWS), :], kbuf[b, s, 0])

        ahead = score(items[0])
        for i, (g, b, s, k) in enumerate(items):
            now = ahead
            if i + 1 < len(items):
                ahead = score(items[i + 1])
            rows = pl.ds(k * CROWS, CROWS)
            if first:
                m, acc = jnp.full((CROWS, HD), NEG, F32), None
            else:
                m, acc = m_ref[g, s, rows, :], acc_ref[g, s, rows, :]
            m, acc = fold(now, kbuf[b, s, 1], bias[g, b, s], m, acc)
            m_ref[g, s, rows, :] = m
            acc_ref[g, s, rows, :] = acc
            if done is not None and k == CH - 1:
                done(g, s)

    def o_copies(g, s):
        return (
            remote(osend.at[g, s], orecv.at[4 - g, s], o_ss.at[g, s], o_rs.at[4 - g, s], at_y(g)),
            remote(lsend.at[g, s], lrecv.at[4 - g, s], l_ss.at[g, s], l_rs.at[4 - g, s], at_y(g)),
        )

    def send_o(g, s):
        total = acc_ref[g, s, :, HD:]
        safe = jnp.where(total > 0, total, 1.0)
        osend[g, s] = (acc_ref[g, s, :, :HD] / safe).astype(BF16)
        log = m_ref[g, s] + jnp.log2(safe)
        lsend[g, s] = jnp.transpose(log)[0:8]
        for copy in o_copies(g, s):
            copy.start()

    for s in range(2):
        kc[0][s].wait_recv()
    temporal([(0, 0, 0), (0, 0, 1)], True)
    kx[0].wait_send()
    start(kx[1])
    up[0].wait_recv()
    far = [start(query_copy(3, 2, 0, 1)), None]
    down[1].wait_recv()
    far[1] = start(query_copy(1, 2, 1, 3))
    down[0].wait_recv()
    up[1].wait_recv()
    for g in (1, 3, 2):
        tx[4 - g].wait_recv()
        spread(trecv[g], g)
    h_next = start(remote(wbuf.at[:, :, pl.ds(2 * TILE, TILE)], wbuf.at[:, :, pl.ds(0, TILE)],
                          h_ss.at[0], h_rs.at[0], after))
    h_prev = start(remote(wbuf.at[:, :, pl.ds(TILE, TILE)], wbuf.at[:, :, pl.ds(3 * TILE, TILE)],
                          h_ss.at[1], h_rs.at[1], before))
    temporal([(1, 0, 0), (1, 0, 1)], True)
    kx[0].wait_recv()
    start(kc[1][0])
    temporal([(3, 0, 0), (3, 0, 1)], True)
    for copy in far:
        copy.wait_recv()
    temporal([(2, 0, 0), (2, 0, 1)], True)
    kc[1][0].wait_recv()
    kx[1].wait_recv()
    start(kc[1][1])
    load_w.wait()
    mine = pl.ds(pl.multiple_of(c * WROWS, 16), WROWS)
    w_cross = start(remote(w_ref.at[mine, pl.ds(EW, CE)], wx.at[mine], wx_ss.at[0], wx_rs.at[0], x_other))
    w_core = remote(wx.at[mine], wx.at[mine], wx_ss.at[1], wx_rs.at[1], core)
    temporal([(g, 1, 0) for g in (2, 1, 3)], False, send_o)
    kc[1][1].wait_recv()
    temporal([(g, 1, 1) for g in (2, 1, 3)], False, send_o)
    temporal([(0, 1, 0), (0, 1, 1)], False)

    h_next.wait_recv()
    h_prev.wait_recv()

    window_bias = [
        rows_bias(lambda half, t=t: window[half][t : t + 1, :]) for t in range(4)
    ]
    items = [(s, k) for s in range(3) for k in range(CH)]
    ahead = scores(qslide[0, 0:CROWS, :], wbuf[0, 0])
    for i, (s, k) in enumerate(items):
        now = ahead
        if i + 1 < len(items):
            s1, k1 = items[i + 1]
            ahead = scores(qslide[s1, k1 * CROWS : (k1 + 1) * CROWS, :], wbuf[s1, 0])
        _, acc = fold(now, wbuf[s, 1], window_bias, jnp.full((CROWS, HD), NEG, F32), None)
        attn[k, :, (s + 2) * HD : (s + 3) * HD] = (acc[:, :HD] / acc[:, HD:]).astype(BF16)

    def combine(k):
        rows = pl.ds(k * CROWS, CROWS)
        for s in range(2):
            total = acc_ref[0, s, rows, HD:]
            logs = [m_ref[0, s, rows, :] + jnp.log2(total)]
            outs = [acc_ref[0, s, rows, :HD] / total]
            for g in range(1, 4):
                line = lrecv[g, s, 0:1, k * CROWS : (k + 1) * CROWS]
                logs.append(jnp.transpose(jnp.broadcast_to(line, (HD, CROWS))))
                outs.append(orecv[g, s, rows, :].astype(F32))
            top = functools.reduce(jnp.maximum, logs)
            weights = [jnp.exp2(log - top) for log in logs]
            mixed = functools.reduce(jnp.add, [w * o for w, o in zip(weights, outs)])
            attn[k, :, s * HD : (s + 1) * HD] = (
                mixed / functools.reduce(jnp.add, weights)
            ).astype(BF16)

    WIDTH = 768

    def reorder(k):
        slots = [attn[k, :, s * HD : (s + 1) * HD] for s in range(5)]
        for i in range(5):
            value = slots[0]
            for s in range(1, 5):
                if i in heads_of[s]:
                    value = lax.select(order[s] == i, slots[s], value)
            attn[k, :, i * HD : (i + 1) * HD] = value

    def project(k, first, last):
        whole = (last - first) // WIDTH

        @pl.loop(0, whole)
        def _(j):
            columns = pl.ds(pl.multiple_of(first + j * WIDTH, 128), WIDTH)
            pbuf[k, :, columns] = dot(attn[k], w_ref[:, columns], 1, 0).astype(BF16)

        rest = first + whole * WIDTH
        if rest < last:
            pbuf[k, :, rest:last] = dot(attn[k], w_ref[:, rest:last], 1, 0).astype(BF16)

    def exchange(k):
        for zr in range(4):
            at = (zr * 2 + 1) * DROWS
            asend[k, zr * DROWS : (zr + 1) * DROWS, :] = attn[k, at : at + DROWS, :]
        return start(remote(asend.at[k], arecv.at[k], a_ss.at[k], a_rs.at[k], x_other))

    def project_two(k):
        kept = jnp.concatenate(
            [attn[k, zr * ZROWS : zr * ZROWS + DROWS, :] for zr in range(4)], axis=0
        )

        @pl.loop(0, CE // 512)
        def _(j):
            columns = pl.ds(pl.multiple_of(EW + j * 512, 512), 512)
            others = pl.ds(pl.multiple_of(j * 512, 512), 512)
            value = dot(kept, w_ref[:, columns], 1, 0) + dot(arecv[k], wx[:, others], 1, 0)
            value = value.astype(BF16)
            for zr in range(4):
                pbuf[k, zr * ZROWS : zr * ZROWS + DROWS, columns] = value[zr * DROWS : (zr + 1) * DROWS]

    def block(k, zr, xr, first, width):
        return pbuf.at[k, pl.ds((zr * 2 + xr) * DROWS, DROWS), pl.ds(first, width)]

    def add(k, zr, xr, first, width, *others):
        @pl.loop(0, DROWS // 16)
        def _(i):
            rows = pl.ds(pl.multiple_of((zr * 2 + xr) * DROWS + i * 16, 16), 16)
            value = pbuf[k, rows, first : first + width].astype(F32)
            for other in others:
                value += other[pl.ds(pl.multiple_of(i * 16, 16), 16), :].astype(F32)
            pbuf[k, rows, first : first + width] = value.astype(BF16)

    def emit(k, first, width, *others):
        @pl.loop(0, DROWS // 16)
        def _(i):
            value = pbuf[k, pl.ds(pl.multiple_of(i * 16, 16), 16), first : first + width].astype(F32)
            for other in others:
                value += other[pl.ds(pl.multiple_of(i * 16, 16), 16), :].astype(F32)
            rows = pl.ds(pl.multiple_of(k * DROWS + i * 16, 16), 16)
            out_ref[rows, first : first + width] = value.astype(BF16)

    H1, H2 = CA, CA + HB

    class Chunk:
        def __init__(self, k):
            self.k = k
            self.count = 0

        def send(self, src, dst, peer):
            n = self.count
            self.count += 1
            return start(remote(src, dst, r_ss.at[self.k, n], r_rs.at[self.k, n], peer))

        def first_a(self):
            k = self.k
            self.fa = [
                self.send(block(k, 2, 0, 0, CA), fa.at[k, 0], z_up),
                self.send(block(k, 2, 1, 0, CA), fa.at[k, 1], z_down),
            ]
            self.ra = [
                self.send(block(k, 1, 1, 0, CA), ra.at[k, 0, 1], z_up),
                self.send(block(k, 3, 0, 0, CA), ra.at[k, 1, 0], z_down),
            ]

        def first_b(self):
            k = self.k
            self.xb = {}
            for zr in (2, 1, 3, 0):
                self.xb[zr] = self.send(block(k, zr, 1, CA, CB), xb.at[k, zr], x_other)

        def forward_a(self):
            k = self.k
            self.fa[0].wait_recv()
            add(k, 1, 0, 0, CA, fa.at[k, 0])
            self.ra.append(self.send(block(k, 1, 0, 0, CA), ra.at[k, 0, 0], z_up))
            self.fa[1].wait_recv()
            add(k, 3, 1, 0, CA, fa.at[k, 1])
            self.ra.append(self.send(block(k, 3, 1, 0, CA), ra.at[k, 1, 1], z_down))

        def second_b(self):
            k = self.k
            self.xb[2].wait_recv()
            add(k, 2, 0, CA, CB, xb.at[k, 2])
            self.fb = [
                self.send(block(k, 2, 0, H1, HB), fb.at[k, 0], z_up),
                self.send(block(k, 2, 0, H2, HB), fb.at[k, 1], z_down),
            ]
            self.xb[1].wait_recv()
            add(k, 1, 0, CA, CB, xb.at[k, 1])
            self.rb = [self.send(block(k, 1, 0, H2, HB), rb.at[k, 0, 1], z_up)]
            self.xb[3].wait_recv()
            add(k, 3, 0, CA, CB, xb.at[k, 3])
            self.rb.append(self.send(block(k, 3, 0, H1, HB), rb.at[k, 1, 0], z_down))

        def first_e(self):
            k = self.k
            self.fe = [
                self.send(block(k, 2, 0, EW, HE), fe.at[k, 0], z_up),
                self.send(block(k, 2, 0, EW + HE, HE), fe.at[k, 1], z_down),
            ]
            self.re = [
                self.send(block(k, 1, 0, EW + HE, HE), re.at[k, 0, 1], z_up),
                self.send(block(k, 3, 0, EW, HE), re.at[k, 1, 0], z_down),
            ]

        def forward_e(self):
            k = self.k
            self.fe[0].wait_recv()
            add(k, 1, 0, EW, HE, fe.at[k, 0])
            self.re.append(self.send(block(k, 1, 0, EW, HE), re.at[k, 0, 0], z_up))
            self.fe[1].wait_recv()
            add(k, 3, 0, EW + HE, HE, fe.at[k, 1])
            self.re.append(self.send(block(k, 3, 0, EW + HE, HE), re.at[k, 1, 1], z_down))

        def finish_e(self):
            k = self.k
            for copy in self.re:
                copy.wait_recv()
            emit(k, EW, HE, re.at[k, 0, 0], re.at[k, 1, 0])
            emit(k, EW + HE, HE, re.at[k, 0, 1], re.at[k, 1, 1])

        def third_a(self):
            k = self.k
            for copy in self.ra:
                copy.wait_recv()
            add(k, 0, 1, 0, CA, ra.at[k, 0, 1], ra.at[k, 1, 1])
            self.xa = self.send(block(k, 0, 1, 0, CA), xa.at[k], x_other)

        def forward_b(self):
            k = self.k
            self.fb[0].wait_recv()
            add(k, 1, 0, H1, HB, fb.at[k, 0])
            self.rb.append(self.send(block(k, 1, 0, H1, HB), rb.at[k, 0, 0], z_up))
            self.fb[1].wait_recv()
            add(k, 3, 0, H2, HB, fb.at[k, 1])
            self.rb.append(self.send(block(k, 3, 0, H2, HB), rb.at[k, 1, 1], z_down))

        def finish(self):
            k = self.k
            self.xa.wait_recv()
            emit(k, 0, CA, ra.at[k, 0, 0], ra.at[k, 1, 0], xa.at[k])
            self.xb[0].wait_recv()
            for copy in self.rb:
                copy.wait_recv()
            emit(k, H1, HB, xb.at[k, 0, :, pl.ds(0, HB)], rb.at[k, 0, 0], rb.at[k, 1, 0])
            emit(k, H2, HB, xb.at[k, 0, :, pl.ds(HB, HB)], rb.at[k, 0, 1], rb.at[k, 1, 1])

    one, two = Chunk(0), Chunk(1)
    for g in (1, 3, 2):
        for s in range(2):
            for copy in o_copies(4 - g, s):
                copy.wait_recv()
    combine(0)
    reorder(0)
    crossed = [exchange(0)]
    project(0, CA, EW)
    one.first_b()
    project(0, 0, CA)
    one.first_a()
    w_cross.wait_recv()
    start(w_core)
    combine(1)
    reorder(1)
    crossed.append(exchange(1))
    project(1, CA, EW)
    two.first_b()
    project(1, 0, CA)
    two.first_a()
    w_core.wait_recv()
    crossed[0].wait_recv()
    project_two(0)
    one.first_e()
    one.forward_a()
    crossed[1].wait_recv()
    project_two(1)
    two.first_e()
    two.forward_a()
    one.forward_e()
    one.second_b()
    one.third_a()
    two.forward_e()
    one.forward_b()
    two.second_b()
    two.third_a()
    two.forward_b()
    one.finish_e()
    two.finish_e()
    one.finish()
    two.finish()

    for copy in sent:
        copy.wait_send()
    for g in range(1, 4):
        for s in range(2):
            for copy in o_copies(g, s):
                copy.wait_send()


def per_device(queries, keys_values, head_kind, tile_neighbours, tile_mask, out_weight):
    smem = pl.BlockSpec(memory_space=pltpu.SMEM)
    vmem = pl.BlockSpec(memory_space=pltpu.VMEM)
    dma = pltpu.SemaphoreType.DMA
    return pl.pallas_call(
        kernel,
        out_shape=jax.ShapeDtypeStruct((ROWS // 8, D), BF16),
        in_specs=[
            smem, smem, smem,
            vmem, vmem,
            pl.BlockSpec(memory_space=pl.ANY),
        ],
        out_specs=vmem,
        scratch_shapes=[
            pltpu.VMEM((5 * HD, D), BF16),
            pltpu.VMEM((4, 2, ROWS, HD), BF16),
            pltpu.VMEM((3, ROWS, HD), BF16),
            pltpu.VMEM((2, 2, 2, 2 * ROWS, HD), BF16),
            pltpu.VMEM((3, 2, 4 * TILE, HD), BF16),
            pltpu.VMEM((8, HD), F32),
            pltpu.VMEM((4, 8, HD), F32),
            pltpu.VMEM((4, 4, 32, HD), F32),
            pltpu.VMEM((4, 2, ROWS, HD), F32),
            pltpu.VMEM((4, 2, ROWS, 2 * HD), F32),
            pltpu.VMEM((4, 2, ROWS, HD), BF16),
            pltpu.VMEM((4, 2, 8, ROWS), F32),
            pltpu.VMEM((4, 2, ROWS, HD), BF16),
            pltpu.VMEM((4, 2, 8, ROWS), F32),
            pltpu.VMEM((CH, CROWS, 5 * HD), BF16),
            pltpu.VMEM((CH, CROWS, D), BF16),
            pltpu.VMEM((CH, 2, DROWS, CA), BF16),
            pltpu.VMEM((CH, 2, 2, DROWS, CA), BF16),
            pltpu.VMEM((CH, DROWS, CA), BF16),
            pltpu.VMEM((CH, 4, DROWS, CB), BF16),
            pltpu.VMEM((CH, 2, DROWS, HB), BF16),
            pltpu.VMEM((CH, 2, 2, DROWS, HB), BF16),
            pltpu.VMEM((5 * HD, CE), BF16),
            pltpu.VMEM((CH, CROWS // 2, 5 * HD), BF16),
            pltpu.VMEM((CH, CROWS // 2, 5 * HD), BF16),
            pltpu.VMEM((CH, 2, DROWS, HE), BF16),
            pltpu.VMEM((CH, 2, 2, DROWS, HE), BF16),
            dma,
            dma((4, 2)), dma((4, 2)),
            dma((4,)), dma((4,)),
            dma((2,)), dma((2,)),
            dma((2, 2)), dma((2, 2)),
            dma((2,)), dma((2,)),
            dma((4, 2)), dma((4, 2)),
            dma((4, 2)), dma((4, 2)),
            dma((CH, 30)), dma((CH, 30)),
            dma((2,)), dma((2,)),
            dma((CH,)), dma((CH,)),
        ],
        name="attend_project",
        compiler_params=pltpu.CompilerParams(
            collective_id=0, has_side_effects=True, vmem_limit_bytes=60 * 2**20
        ),
    )(
        head_kind,
        tile_neighbours,
        tile_mask,
        jnp.transpose(queries, (1, 0, 2)),
        jnp.transpose(keys_values, (0, 2, 1, 3)),
        out_weight,
    )


def solution(mesh):
    return jax.shard_map(
        per_device,
        mesh=mesh,
        in_specs=(
            P("frame", "head", None),
            P(None, "frame", "head", None),
            P("head"),
            P("frame", None),
            P("frame", None),
            P("head", None),
        ),
        out_specs=P(("frame", "head"), None),
        check_vma=False,
    )
```

```python
import functools
import math

import jax
import jax.numpy as jnp
from jax import lax
from jax.experimental import pallas as pl
from jax.experimental.pallas import tpu as pltpu
from jax.sharding import PartitionSpec as P

MESH = pl.DeviceIdType.MESH
F32 = jnp.float32
BF16 = jnp.bfloat16

ROWS = 768
TILE = 384
HD = 128
D = 5120
CH = 2
CROWS = ROWS // CH
DROWS = CROWS // 8
ZROWS = 2 * DROWS
CA = 2048
CB = 1024
CE = D - CA - CB
EW = CA + CB
HB, HE = CB // 2, CE // 2
WROWS = 5 * HD // 2
NEG = -1e30
OFF = -2e30
SCALE = HD**-0.5 * math.log2(math.e)


def dot(a, b, ca, cb):
    return lax.dot_general(a, b, (((ca,), (cb,)), ((), ())), preferred_element_type=F32)


def scores(q, k):
    scaled = q.astype(F32) * SCALE
    high = scaled.astype(BF16)
    low = (scaled - high.astype(F32)).astype(BF16)
    return dot(jnp.concatenate([high, low], axis=1), jnp.concatenate([k, k], axis=1), 1, 1)


def fold(s, v, bias, m, acc):
    tiles = len(bias)
    rows = s.shape[0]
    new = m
    for t in range(tiles):
        part = s[:, t * TILE : (t + 1) * TILE]
        top = jnp.broadcast_to(jnp.max(part, axis=1, keepdims=True), (rows, HD))
        new = jnp.maximum(new, top + bias[t])
    pieces = []
    for t in range(tiles):
        sub = new - bias[t]
        for u in range(TILE // HD):
            at = t * TILE + u * HD
            pieces.append(jnp.exp2(s[:, at : at + HD] - sub).astype(BF16))
    o = dot(jnp.concatenate(pieces, axis=1), jnp.concatenate([v, jnp.ones_like(v)], axis=1), 1, 0)
    if acc is None:
        return new, o
    f = jnp.exp2(m - new)
    return new, acc * jnp.concatenate([f, f], axis=1) + o


def kernel(
    kind_ref, near_ref, mask_ref, q_ref, kv_ref, w_hbm, out_ref,
    w_ref, qall, qslide, kbuf, wbuf, tsend, trecv, tab, m_ref, acc_ref,
    osend, lsend, orecv, lrecv, attn, pbuf,
    fa, ra, xa, xb, fb, rb, wx, asend, arecv, fe, re,
    w_sem, q_ss, q_rs, t_ss, t_rs, kx_ss, kx_rs, kc_ss, kc_rs, h_ss, h_rs,
    o_ss, o_rs, l_ss, l_rs, r_ss, r_rs, wx_ss, wx_rs, a_ss, a_rs,
):
    frame = lax.axis_index("frame")
    head = lax.axis_index("head")
    xl, y, c = frame // 8, (frame // 2) % 4, frame % 2
    z, xh = head // 2, head % 2

    def frame_of(a, b, d):
        return (a * 4 + b) * 2 + d

    def at_y(g):
        return (frame_of(xl, (y + g) % 4, c), head)

    core = (frame_of(xl, y, 1 - c), head)
    across = (frame_of(1 - xl, y, c), head)
    after = ((frame + 1) % 16, head)
    before = ((frame + 15) % 16, head)
    z_up = (frame, ((z + 1) % 4) * 2 + xh)
    z_down = (frame, ((z + 3) % 4) * 2 + xh)
    x_other = (frame, z * 2 + 1 - xh)

    load_w = pltpu.make_async_copy(w_hbm, w_ref, w_sem)
    load_w.start()

    barrier = pltpu.get_barrier_semaphore()
    peers = [at_y(1), at_y(2), at_y(3), core, across, after, before, z_up, z_down, x_other]
    for peer in peers:
        pl.semaphore_signal(barrier, inc=1, device_id=peer, device_id_type=MESH)
    pl.semaphore_wait(barrier, len(peers))

    def remote(src, dst, ss, rs, peer):
        return pltpu.make_async_remote_copy(
            src_ref=src, dst_ref=dst, send_sem=ss, recv_sem=rs, device_id=peer, device_id_type=MESH
        )

    sent = []

    def start(copy):
        copy.start()
        sent.append(copy)
        return copy

    kinds = [kind_ref[i] for i in range(5)]
    many = functools.reduce(jnp.add, kinds)
    order = [0] * 5
    seen = 0
    for i in range(5):
        slot = jnp.where(kinds[i] == 1, seen, many + i - seen)
        seen = seen + kinds[i]
        order = [jnp.where(slot == s, i, order[s]) for s in range(5)]
    heads_of = [range(5), range(5), range(0, 3), range(1, 4), range(2, 5)]

    def choose(s, get):
        value = get(heads_of[s][0])
        for i in heads_of[s][1:]:
            value = lax.select(order[s] == i, get(i), value)
        return value

    @pl.loop(0, ROWS // 96)
    def _(r):
        rows = pl.ds(pl.multiple_of(r * 96, 96), 96)
        for s in range(2):
            for t in range(2):
                kbuf[0, s, t, rows, :] = choose(s, lambda i: kv_ref[t, i, rows, :])

    kx = [
        start(remote(kbuf.at[0, s, :, pl.ds(0, ROWS)], kbuf.at[1, s, :, pl.ds(0, ROWS)],
                     kx_ss.at[s], kx_rs.at[s], across))
        for s in range(2)
    ]
    kc = [
        [remote(kbuf.at[b, s, :, pl.ds(0, ROWS)], kbuf.at[b, s, :, pl.ds(ROWS, ROWS)],
                kc_ss.at[b, s], kc_rs.at[b, s], core) for s in range(2)]
        for b in range(2)
    ]
    for s in range(2):
        start(kc[0][s])
    def stage_queries(slots, store):
        for k in range(CH):

            @pl.loop(0, 8)
            def _(d):
                dest = ((z + d // 2) % 4) * 2 + (xh + d % 2) % 2
                rows = pl.ds(pl.multiple_of((dest * CH + k) * DROWS, 16), DROWS)
                to = pl.ds(pl.multiple_of(k * CROWS + d * DROWS, 16), DROWS)
                for s in slots:
                    store(s, to, choose(s, lambda i: q_ref[i, rows, :]))

    def store_temporal(s, to, value):
        qall[0, s, to, :] = value

    def store_sliding(s, to, value):
        qslide[s - 2, to, :] = value

    stage_queries(range(2), store_temporal)

    def allowed(half, ids):
        hit = ids == frame * 2 + half
        for n in range(2):
            listed = jnp.where(mask_ref[half, n] == 1, near_ref[half, n], -5)
            hit = hit | (ids == listed)
        return hit

    lane_ids = lax.broadcasted_iota(jnp.int32, (1, HD), 1)
    for s in range(2):
        shift = jnp.where(s < many, 0.0, OFF)
        for half in range(2):
            tsend[s * 2 + half : s * 2 + half + 1, :] = jnp.where(allowed(half, lane_ids), 0.0, shift)
    tsend[4:8, :] = jnp.zeros((4, HD), F32)
    window_ids = frame * 2 - 1 + lax.broadcasted_iota(jnp.int32, (8, HD), 0)
    window = [jnp.where(allowed(half, window_ids), 0.0, OFF) for half in range(2)]

    def query_copy(src, dst, s, g):
        return remote(qall.at[src, s], qall.at[dst, s], q_ss.at[dst, s], q_rs.at[dst, s], at_y(g))

    up = [start(query_copy(0, 3, 0, 1)), None]
    down = [None, start(query_copy(0, 1, 1, 3))]
    up[1] = start(query_copy(0, 3, 1, 1))
    down[0] = start(query_copy(0, 1, 0, 3))
    tx = [None] * 4
    for g in (1, 3, 2):
        tx[g] = start(remote(tsend, trecv.at[4 - g], t_ss.at[g], t_rs.at[4 - g], at_y(g)))

    @pl.loop(0, ROWS // 96)
    def _(r):
        rows = pl.ds(pl.multiple_of(r * 96, 96), 96)
        to = pl.ds(pl.multiple_of(TILE + r * 96, 96), 96)
        for s in range(3):
            for t in range(2):
                wbuf[s, t, to, :] = choose(s + 2, lambda i: kv_ref[t, i, rows, :])

    def spread(src, g):
        for i in range(4):
            row = jnp.broadcast_to(src[i : i + 1, :], (128, 128))
            tab[g, i] = jnp.transpose(row)[0:32]

    spread(tsend[...], 0)
    stage_queries(range(2, 5), store_sliding)

    half_of = [((z + zr) % 4) // 2 for zr in range(4)]

    def rows_bias(get):
        low, high = get(0), get(1)
        blocks = []
        for zr in range(4):
            pick = jnp.where(half_of[zr] == 0, low, high)
            blocks.append(jnp.broadcast_to(pick, (ZROWS, HD)))
        return jnp.concatenate(blocks, axis=0)

    def temporal_bias(g, s, b):
        bias = []
        for d in range(2):
            part = frame_of(xl if b == 0 else 1 - xl, y, c if d == 0 else 1 - c)
            for t in range(2):
                bias.append(rows_bias(lambda half: tab[g, s * 2 + half, pl.ds(part * 2 + t, 1), :]))
        return bias

    def temporal(g, b, chunks, first, done=None):
        items = [(s, k) for s in range(2) for k in chunks]
        bias = [temporal_bias(g, s, b) for s in range(2)]

        def score(item):
            s, k = item
            return scores(qall[g, s, pl.ds(k * CROWS, CROWS), :], kbuf[b, s, 0])

        ahead = score(items[0])
        for i, (s, k) in enumerate(items):
            now = ahead
            if i + 1 < len(items):
                ahead = score(items[i + 1])
            rows = pl.ds(k * CROWS, CROWS)
            if first:
                m, acc = jnp.full((CROWS, HD), NEG, F32), None
            else:
                m, acc = m_ref[g, s, rows, :], acc_ref[g, s, rows, :]
            m, acc = fold(now, kbuf[b, s, 1], bias[s], m, acc)
            m_ref[g, s, rows, :] = m
            acc_ref[g, s, rows, :] = acc
            if done is not None and k == CH - 1:
                done(s)

    def o_copies(g, s):
        return (
            remote(osend.at[g, s], orecv.at[4 - g, s], o_ss.at[g, s], o_rs.at[4 - g, s], at_y(g)),
            remote(lsend.at[g, s], lrecv.at[4 - g, s], l_ss.at[g, s], l_rs.at[4 - g, s], at_y(g)),
        )

    def send_o(g, s):
        total = acc_ref[g, s, :, HD:]
        safe = jnp.where(total > 0, total, 1.0)
        osend[g, s] = (acc_ref[g, s, :, :HD] / safe).astype(BF16)
        log = m_ref[g, s] + jnp.log2(safe)
        lsend[g, s] = jnp.transpose(log)[0:8]
        for copy in o_copies(g, s):
            copy.start()

    for s in range(2):
        kc[0][s].wait_recv()
    temporal(0, 0, range(CH), True)
    up[0].wait_recv()
    far = [start(query_copy(3, 2, 0, 1)), None]
    down[1].wait_recv()
    far[1] = start(query_copy(1, 2, 1, 3))
    down[0].wait_recv()
    up[1].wait_recv()
    for g in (1, 3, 2):
        tx[4 - g].wait_recv()
        spread(trecv[g], g)
    h_next = start(remote(wbuf.at[:, :, pl.ds(2 * TILE, TILE)], wbuf.at[:, :, pl.ds(0, TILE)],
                          h_ss.at[0], h_rs.at[0], after))
    h_prev = start(remote(wbuf.at[:, :, pl.ds(TILE, TILE)], wbuf.at[:, :, pl.ds(3 * TILE, TILE)],
                          h_ss.at[1], h_rs.at[1], before))
    temporal(1, 0, range(CH), True)
    temporal(3, 0, range(CH), True)
    for s in range(2):
        kx[s].wait_recv()
        start(kc[1][s])
    load_w.wait()
    mine = pl.ds(pl.multiple_of(c * WROWS, 16), WROWS)
    w_cross = start(remote(w_ref.at[mine, pl.ds(EW, CE)], wx.at[mine], wx_ss.at[0], wx_rs.at[0], x_other))
    w_core = remote(wx.at[mine], wx.at[mine], wx_ss.at[1], wx_rs.at[1], core)
    for copy in far:
        copy.wait_recv()
    temporal(2, 0, range(CH), True)
    for s in range(2):
        kc[1][s].wait_recv()

    @pl.loop(0, 2)
    def _(i):
        g = 1 + 2 * i
        temporal(g, 1, range(CH), False)
        for s in range(2):
            send_o(g, s)

    temporal(2, 1, range(CH), False, lambda s: send_o(2, s))
    temporal(0, 1, range(CH), False)

    h_next.wait_recv()
    h_prev.wait_recv()

    window_bias = [
        rows_bias(lambda half, t=t: window[half][t : t + 1, :]) for t in range(4)
    ]
    items = [(s, k) for s in range(3) for k in range(CH)]
    ahead = scores(qslide[0, 0:CROWS, :], wbuf[0, 0])
    for i, (s, k) in enumerate(items):
        now = ahead
        if i + 1 < len(items):
            s1, k1 = items[i + 1]
            ahead = scores(qslide[s1, k1 * CROWS : (k1 + 1) * CROWS, :], wbuf[s1, 0])
        _, acc = fold(now, wbuf[s, 1], window_bias, jnp.full((CROWS, HD), NEG, F32), None)
        attn[k, :, (s + 2) * HD : (s + 3) * HD] = (acc[:, :HD] / acc[:, HD:]).astype(BF16)

    def combine(k):
        rows = pl.ds(k * CROWS, CROWS)
        for s in range(2):
            total = acc_ref[0, s, rows, HD:]
            logs = [m_ref[0, s, rows, :] + jnp.log2(total)]
            outs = [acc_ref[0, s, rows, :HD] / total]
            for g in range(1, 4):
                line = lrecv[g, s, 0:1, k * CROWS : (k + 1) * CROWS]
                logs.append(jnp.transpose(jnp.broadcast_to(line, (HD, CROWS))))
                outs.append(orecv[g, s, rows, :].astype(F32))
            top = functools.reduce(jnp.maximum, logs)
            weights = [jnp.exp2(log - top) for log in logs]
            mixed = functools.reduce(jnp.add, [w * o for w, o in zip(weights, outs)])
            attn[k, :, s * HD : (s + 1) * HD] = (
                mixed / functools.reduce(jnp.add, weights)
            ).astype(BF16)

    WIDTH = 768

    def reorder(k):
        slots = [attn[k, :, s * HD : (s + 1) * HD] for s in range(5)]
        for i in range(5):
            value = slots[0]
            for s in range(1, 5):
                if i in heads_of[s]:
                    value = lax.select(order[s] == i, slots[s], value)
            attn[k, :, i * HD : (i + 1) * HD] = value

    def project(k, first, last):
        whole = (last - first) // WIDTH

        @pl.loop(0, whole)
        def _(j):
            columns = pl.ds(pl.multiple_of(first + j * WIDTH, 128), WIDTH)
            pbuf[k, :, columns] = dot(attn[k], w_ref[:, columns], 1, 0).astype(BF16)

        rest = first + whole * WIDTH
        if rest < last:
            pbuf[k, :, rest:last] = dot(attn[k], w_ref[:, rest:last], 1, 0).astype(BF16)

    def exchange(k):
        for zr in range(4):
            at = (zr * 2 + 1) * DROWS
            asend[k, zr * DROWS : (zr + 1) * DROWS, :] = attn[k, at : at + DROWS, :]
        return start(remote(asend.at[k], arecv.at[k], a_ss.at[k], a_rs.at[k], x_other))

    def project_two(k):
        kept = jnp.concatenate(
            [attn[k, zr * ZROWS : zr * ZROWS + DROWS, :] for zr in range(4)], axis=0
        )

        @pl.loop(0, CE // 512)
        def _(j):
            columns = pl.ds(pl.multiple_of(EW + j * 512, 512), 512)
            others = pl.ds(pl.multiple_of(j * 512, 512), 512)
            value = dot(kept, w_ref[:, columns], 1, 0) + dot(arecv[k], wx[:, others], 1, 0)
            value = value.astype(BF16)
            for zr in range(4):
                pbuf[k, zr * ZROWS : zr * ZROWS + DROWS, columns] = value[zr * DROWS : (zr + 1) * DROWS]

    def block(k, zr, xr, first, width):
        return pbuf.at[k, pl.ds((zr * 2 + xr) * DROWS, DROWS), pl.ds(first, width)]

    def add(k, zr, xr, first, width, *others):
        @pl.loop(0, DROWS // 16)
        def _(i):
            rows = pl.ds(pl.multiple_of((zr * 2 + xr) * DROWS + i * 16, 16), 16)
            value = pbuf[k, rows, first : first + width].astype(F32)
            for other in others:
                value += other[pl.ds(pl.multiple_of(i * 16, 16), 16), :].astype(F32)
            pbuf[k, rows, first : first + width] = value.astype(BF16)

    def emit(k, first, width, *others):
        @pl.loop(0, DROWS // 16)
        def _(i):
            value = pbuf[k, pl.ds(pl.multiple_of(i * 16, 16), 16), first : first + width].astype(F32)
            for other in others:
                value += other[pl.ds(pl.multiple_of(i * 16, 16), 16), :].astype(F32)
            rows = pl.ds(pl.multiple_of(k * DROWS + i * 16, 16), 16)
            out_ref[rows, first : first + width] = value.astype(BF16)

    H1, H2 = CA, CA + HB

    class Chunk:
        def __init__(self, k):
            self.k = k
            self.count = 0

        def send(self, src, dst, peer):
            n = self.count
            self.count += 1
            return start(remote(src, dst, r_ss.at[self.k, n], r_rs.at[self.k, n], peer))

        def first_a(self):
            k = self.k
            self.fa = [
                self.send(block(k, 2, 0, 0, CA), fa.at[k, 0], z_up),
                self.send(block(k, 2, 1, 0, CA), fa.at[k, 1], z_down),
            ]
            self.ra = [
                self.send(block(k, 1, 1, 0, CA), ra.at[k, 0, 1], z_up),
                self.send(block(k, 3, 0, 0, CA), ra.at[k, 1, 0], z_down),
            ]

        def first_b(self):
            k = self.k
            self.xb = {}
            for zr in (2, 1, 3, 0):
                self.xb[zr] = self.send(block(k, zr, 1, CA, CB), xb.at[k, zr], x_other)

        def forward_a(self):
            k = self.k
            self.fa[0].wait_recv()
            add(k, 1, 0, 0, CA, fa.at[k, 0])
            self.ra.append(self.send(block(k, 1, 0, 0, CA), ra.at[k, 0, 0], z_up))
            self.fa[1].wait_recv()
            add(k, 3, 1, 0, CA, fa.at[k, 1])
            self.ra.append(self.send(block(k, 3, 1, 0, CA), ra.at[k, 1, 1], z_down))

        def second_b(self):
            k = self.k
            self.xb[2].wait_recv()
            add(k, 2, 0, CA, CB, xb.at[k, 2])
            self.fb = [
                self.send(block(k, 2, 0, H1, HB), fb.at[k, 0], z_up),
                self.send(block(k, 2, 0, H2, HB), fb.at[k, 1], z_down),
            ]
            self.xb[1].wait_recv()
            add(k, 1, 0, CA, CB, xb.at[k, 1])
            self.rb = [self.send(block(k, 1, 0, H2, HB), rb.at[k, 0, 1], z_up)]
            self.xb[3].wait_recv()
            add(k, 3, 0, CA, CB, xb.at[k, 3])
            self.rb.append(self.send(block(k, 3, 0, H1, HB), rb.at[k, 1, 0], z_down))

        def first_e(self):
            k = self.k
            self.fe = [
                self.send(block(k, 2, 0, EW, HE), fe.at[k, 0], z_up),
                self.send(block(k, 2, 0, EW + HE, HE), fe.at[k, 1], z_down),
            ]
            self.re = [
                self.send(block(k, 1, 0, EW + HE, HE), re.at[k, 0, 1], z_up),
                self.send(block(k, 3, 0, EW, HE), re.at[k, 1, 0], z_down),
            ]

        def forward_e(self):
            k = self.k
            self.fe[0].wait_recv()
            add(k, 1, 0, EW, HE, fe.at[k, 0])
            self.re.append(self.send(block(k, 1, 0, EW, HE), re.at[k, 0, 0], z_up))
            self.fe[1].wait_recv()
            add(k, 3, 0, EW + HE, HE, fe.at[k, 1])
            self.re.append(self.send(block(k, 3, 0, EW + HE, HE), re.at[k, 1, 1], z_down))

        def finish_e(self):
            k = self.k
            for copy in self.re:
                copy.wait_recv()
            emit(k, EW, HE, re.at[k, 0, 0], re.at[k, 1, 0])
            emit(k, EW + HE, HE, re.at[k, 0, 1], re.at[k, 1, 1])

        def third_a(self):
            k = self.k
            for copy in self.ra:
                copy.wait_recv()
            add(k, 0, 1, 0, CA, ra.at[k, 0, 1], ra.at[k, 1, 1])
            self.xa = self.send(block(k, 0, 1, 0, CA), xa.at[k], x_other)

        def forward_b(self):
            k = self.k
            self.fb[0].wait_recv()
            add(k, 1, 0, H1, HB, fb.at[k, 0])
            self.rb.append(self.send(block(k, 1, 0, H1, HB), rb.at[k, 0, 0], z_up))
            self.fb[1].wait_recv()
            add(k, 3, 0, H2, HB, fb.at[k, 1])
            self.rb.append(self.send(block(k, 3, 0, H2, HB), rb.at[k, 1, 1], z_down))

        def finish(self):
            k = self.k
            self.xa.wait_recv()
            emit(k, 0, CA, ra.at[k, 0, 0], ra.at[k, 1, 0], xa.at[k])
            self.xb[0].wait_recv()
            for copy in self.rb:
                copy.wait_recv()
            emit(k, H1, HB, xb.at[k, 0, :, pl.ds(0, HB)], rb.at[k, 0, 0], rb.at[k, 1, 0])
            emit(k, H2, HB, xb.at[k, 0, :, pl.ds(HB, HB)], rb.at[k, 0, 1], rb.at[k, 1, 1])

    one, two = Chunk(0), Chunk(1)
    for g in (1, 3, 2):
        for s in range(2):
            for copy in o_copies(4 - g, s):
                copy.wait_recv()
    combine(0)
    reorder(0)
    crossed = [exchange(0)]
    project(0, CA, EW)
    one.first_b()
    project(0, 0, CA)
    one.first_a()
    w_cross.wait_recv()
    start(w_core)
    combine(1)
    reorder(1)
    crossed.append(exchange(1))
    project(1, CA, EW)
    two.first_b()
    project(1, 0, CA)
    two.first_a()
    w_core.wait_recv()
    crossed[0].wait_recv()
    project_two(0)
    one.first_e()
    one.forward_a()
    crossed[1].wait_recv()
    project_two(1)
    two.first_e()
    two.forward_a()
    one.forward_e()
    one.second_b()
    one.third_a()
    two.forward_e()
    one.forward_b()
    two.second_b()
    two.third_a()
    two.forward_b()
    one.finish_e()
    two.finish_e()
    one.finish()
    two.finish()

    for copy in sent:
        copy.wait_send()
    for g in range(1, 4):
        for s in range(2):
            for copy in o_copies(g, s):
                copy.wait_send()


def per_device(queries, keys_values, head_kind, tile_neighbours, tile_mask, out_weight):
    smem = pl.BlockSpec(memory_space=pltpu.SMEM)
    vmem = pl.BlockSpec(memory_space=pltpu.VMEM)
    dma = pltpu.SemaphoreType.DMA
    return pl.pallas_call(
        kernel,
        out_shape=jax.ShapeDtypeStruct((ROWS // 8, D), BF16),
        in_specs=[
            smem, smem, smem,
            vmem, vmem,
            pl.BlockSpec(memory_space=pl.ANY),
        ],
        out_specs=vmem,
        scratch_shapes=[
            pltpu.VMEM((5 * HD, D), BF16),
            pltpu.VMEM((4, 2, ROWS, HD), BF16),
            pltpu.VMEM((3, ROWS, HD), BF16),
            pltpu.VMEM((2, 2, 2, 2 * ROWS, HD), BF16),
            pltpu.VMEM((3, 2, 4 * TILE, HD), BF16),
            pltpu.VMEM((8, HD), F32),
            pltpu.VMEM((4, 8, HD), F32),
            pltpu.VMEM((4, 4, 32, HD), F32),
            pltpu.VMEM((4, 2, ROWS, HD), F32),
            pltpu.VMEM((4, 2, ROWS, 2 * HD), F32),
            pltpu.VMEM((4, 2, ROWS, HD), BF16),
            pltpu.VMEM((4, 2, 8, ROWS), F32),
            pltpu.VMEM((4, 2, ROWS, HD), BF16),
            pltpu.VMEM((4, 2, 8, ROWS), F32),
            pltpu.VMEM((CH, CROWS, 5 * HD), BF16),
            pltpu.VMEM((CH, CROWS, D), BF16),
            pltpu.VMEM((CH, 2, DROWS, CA), BF16),
            pltpu.VMEM((CH, 2, 2, DROWS, CA), BF16),
            pltpu.VMEM((CH, DROWS, CA), BF16),
            pltpu.VMEM((CH, 4, DROWS, CB), BF16),
            pltpu.VMEM((CH, 2, DROWS, HB), BF16),
            pltpu.VMEM((CH, 2, 2, DROWS, HB), BF16),
            pltpu.VMEM((5 * HD, CE), BF16),
            pltpu.VMEM((CH, CROWS // 2, 5 * HD), BF16),
            pltpu.VMEM((CH, CROWS // 2, 5 * HD), BF16),
            pltpu.VMEM((CH, 2, DROWS, HE), BF16),
            pltpu.VMEM((CH, 2, 2, DROWS, HE), BF16),
            dma,
            dma((4, 2)), dma((4, 2)),
            dma((4,)), dma((4,)),
            dma((2,)), dma((2,)),
            dma((2, 2)), dma((2, 2)),
            dma((2,)), dma((2,)),
            dma((4, 2)), dma((4, 2)),
            dma((4, 2)), dma((4, 2)),
            dma((CH, 30)), dma((CH, 30)),
            dma((2,)), dma((2,)),
            dma((CH,)), dma((CH,)),
        ],
        name="attend_project",
        compiler_params=pltpu.CompilerParams(
            collective_id=0, has_side_effects=True, vmem_limit_bytes=60 * 2**20
        ),
    )(
        head_kind,
        tile_neighbours,
        tile_mask,
        jnp.transpose(queries, (1, 0, 2)),
        jnp.transpose(keys_values, (0, 2, 1, 3)),
        out_weight,
    )


def solution(mesh):
    return jax.shard_map(
        per_device,
        mesh=mesh,
        in_specs=(
            P("frame", "head", None),
            P(None, "frame", "head", None),
            P("head"),
            P("frame", None),
            P("frame", None),
            P("head", None),
        ),
        out_specs=P(("frame", "head"), None),
        check_vma=False,
    )
```

```python
import functools
import math

import jax
import jax.numpy as jnp
from jax import lax
from jax.experimental import pallas as pl
from jax.experimental.pallas import tpu as pltpu
from jax.sharding import PartitionSpec as P

MESH = pl.DeviceIdType.MESH
F32 = jnp.float32
BF16 = jnp.bfloat16

ROWS = 768
TILE = 384
HD = 128
D = 5120
CH = 2
CROWS = ROWS // CH
DROWS = CROWS // 8
ZROWS = 2 * DROWS
CA = 2048
CB = 1024
CE = D - CA - CB
EW = CA + CB
HB, HE = CB // 2, CE // 2
WROWS = 5 * HD // 2
NEG = -1e30
OFF = -2e30
SCALE = HD**-0.5 * math.log2(math.e)


def dot(a, b, ca, cb):
    return lax.dot_general(a, b, (((ca,), (cb,)), ((), ())), preferred_element_type=F32)


def scores(q, k):
    scaled = q.astype(F32) * SCALE
    high = scaled.astype(BF16)
    low = (scaled - high.astype(F32)).astype(BF16)
    return dot(jnp.concatenate([high, low], axis=1), jnp.concatenate([k, k], axis=1), 1, 1)


def fold(s, v, bias, m, acc):
    tiles = len(bias)
    rows = s.shape[0]
    new = m
    for t in range(tiles):
        part = s[:, t * TILE : (t + 1) * TILE]
        top = jnp.broadcast_to(jnp.max(part, axis=1, keepdims=True), (rows, HD))
        new = jnp.maximum(new, top + bias[t])
    pieces = []
    for t in range(tiles):
        sub = new - bias[t]
        for u in range(TILE // HD):
            at = t * TILE + u * HD
            pieces.append(jnp.exp2(s[:, at : at + HD] - sub).astype(BF16))
    o = dot(jnp.concatenate(pieces, axis=1), jnp.concatenate([v, jnp.ones_like(v)], axis=1), 1, 0)
    if acc is None:
        return new, o
    f = jnp.exp2(m - new)
    return new, acc * jnp.concatenate([f, f], axis=1) + o


def kernel(
    kind_ref, near_ref, mask_ref, q_ref, kv_ref, w_hbm, out_ref,
    w_ref, qall, qslide, kbuf, wbuf, tsend, trecv, tab, m_ref, acc_ref,
    osend, lsend, orecv, lrecv, attn, pbuf,
    fa, ra, xa, xb, fb, rb, wx, asend, arecv, fe, re,
    w_sem, q_ss, q_rs, t_ss, t_rs, kx_ss, kx_rs, kc_ss, kc_rs, h_ss, h_rs,
    o_ss, o_rs, l_ss, l_rs, r_ss, r_rs, wx_ss, wx_rs, a_ss, a_rs,
):
    frame = lax.axis_index("frame")
    head = lax.axis_index("head")
    xl, y, c = frame // 8, (frame // 2) % 4, frame % 2
    z, xh = head // 2, head % 2

    def frame_of(a, b, d):
        return (a * 4 + b) * 2 + d

    def at_y(g):
        return (frame_of(xl, (y + g) % 4, c), head)

    core = (frame_of(xl, y, 1 - c), head)
    across = (frame_of(1 - xl, y, c), head)
    after = ((frame + 1) % 16, head)
    before = ((frame + 15) % 16, head)
    z_up = (frame, ((z + 1) % 4) * 2 + xh)
    z_down = (frame, ((z + 3) % 4) * 2 + xh)
    x_other = (frame, z * 2 + 1 - xh)

    load_w = pltpu.make_async_copy(w_hbm, w_ref, w_sem)
    load_w.start()

    barrier = pltpu.get_barrier_semaphore()
    peers = [at_y(1), at_y(2), at_y(3), core, across, after, before, z_up, z_down, x_other]
    for peer in peers:
        pl.semaphore_signal(barrier, inc=1, device_id=peer, device_id_type=MESH)
    pl.semaphore_wait(barrier, len(peers))

    def remote(src, dst, ss, rs, peer):
        return pltpu.make_async_remote_copy(
            src_ref=src, dst_ref=dst, send_sem=ss, recv_sem=rs, device_id=peer, device_id_type=MESH
        )

    sent = []

    def start(copy):
        copy.start()
        sent.append(copy)
        return copy

    kinds = [kind_ref[i] for i in range(5)]
    many = functools.reduce(jnp.add, kinds)
    order = [0] * 5
    seen = 0
    for i in range(5):
        slot = jnp.where(kinds[i] == 1, seen, many + i - seen)
        seen = seen + kinds[i]
        order = [jnp.where(slot == s, i, order[s]) for s in range(5)]
    heads_of = [range(5), range(5), range(0, 3), range(1, 4), range(2, 5)]

    def choose(s, get):
        value = get(heads_of[s][0])
        for i in heads_of[s][1:]:
            value = lax.select(order[s] == i, get(i), value)
        return value

    @pl.loop(0, ROWS // 96)
    def _(r):
        rows = pl.ds(pl.multiple_of(r * 96, 96), 96)
        for s in range(2):
            for t in range(2):
                kbuf[0, s, t, rows, :] = choose(s, lambda i: kv_ref[t, i, rows, :])

    kx = [
        start(remote(kbuf.at[0, s, :, pl.ds(0, ROWS)], kbuf.at[1, s, :, pl.ds(0, ROWS)],
                     kx_ss.at[s], kx_rs.at[s], across))
        for s in range(2)
    ]
    kc = [
        [remote(kbuf.at[b, s, :, pl.ds(0, ROWS)], kbuf.at[b, s, :, pl.ds(ROWS, ROWS)],
                kc_ss.at[b, s], kc_rs.at[b, s], core) for s in range(2)]
        for b in range(2)
    ]
    for s in range(2):
        start(kc[0][s])
    def stage_queries(slots, store):
        for k in range(CH):

            @pl.loop(0, 8)
            def _(d):
                dest = ((z + d // 2) % 4) * 2 + (xh + d % 2) % 2
                rows = pl.ds(pl.multiple_of((dest * CH + k) * DROWS, 16), DROWS)
                to = pl.ds(pl.multiple_of(k * CROWS + d * DROWS, 16), DROWS)
                for s in slots:
                    store(s, to, choose(s, lambda i: q_ref[i, rows, :]))

    def store_temporal(s, to, value):
        qall[0, s, to, :] = value

    def store_sliding(s, to, value):
        qslide[s - 2, to, :] = value

    stage_queries(range(2), store_temporal)

    def allowed(half, ids):
        hit = ids == frame * 2 + half
        for n in range(2):
            listed = jnp.where(mask_ref[half, n] == 1, near_ref[half, n], -5)
            hit = hit | (ids == listed)
        return hit

    lane_ids = lax.broadcasted_iota(jnp.int32, (1, HD), 1)
    for s in range(2):
        shift = jnp.where(s < many, 0.0, OFF)
        for half in range(2):
            tsend[s * 2 + half : s * 2 + half + 1, :] = jnp.where(allowed(half, lane_ids), 0.0, shift)
    tsend[4:8, :] = jnp.zeros((4, HD), F32)
    window_ids = frame * 2 - 1 + lax.broadcasted_iota(jnp.int32, (8, HD), 0)
    window = [jnp.where(allowed(half, window_ids), 0.0, OFF) for half in range(2)]

    def query_copy(src, dst, s, g):
        return remote(qall.at[src, s], qall.at[dst, s], q_ss.at[dst, s], q_rs.at[dst, s], at_y(g))

    up = [start(query_copy(0, 3, 0, 1)), None]
    down = [None, start(query_copy(0, 1, 1, 3))]
    up[1] = start(query_copy(0, 3, 1, 1))
    down[0] = start(query_copy(0, 1, 0, 3))
    tx = [None] * 4
    for g in (1, 3, 2):
        tx[g] = start(remote(tsend, trecv.at[4 - g], t_ss.at[g], t_rs.at[4 - g], at_y(g)))

    @pl.loop(0, ROWS // 96)
    def _(r):
        rows = pl.ds(pl.multiple_of(r * 96, 96), 96)
        to = pl.ds(pl.multiple_of(TILE + r * 96, 96), 96)
        for s in range(3):
            for t in range(2):
                wbuf[s, t, to, :] = choose(s + 2, lambda i: kv_ref[t, i, rows, :])

    def spread(src, g):
        for i in range(4):
            row = jnp.broadcast_to(src[i : i + 1, :], (128, 128))
            tab[g, i] = jnp.transpose(row)[0:32]

    spread(tsend[...], 0)
    stage_queries(range(2, 5), store_sliding)

    half_of = [((z + zr) % 4) // 2 for zr in range(4)]

    def rows_bias(get):
        low, high = get(0), get(1)
        blocks = []
        for zr in range(4):
            pick = jnp.where(half_of[zr] == 0, low, high)
            blocks.append(jnp.broadcast_to(pick, (ZROWS, HD)))
        return jnp.concatenate(blocks, axis=0)

    def temporal_bias(g, s, b):
        bias = []
        for d in range(2):
            part = frame_of(xl if b == 0 else 1 - xl, y, c if d == 0 else 1 - c)
            for t in range(2):
                bias.append(rows_bias(lambda half: tab[g, s * 2 + half, pl.ds(part * 2 + t, 1), :]))
        return bias

    def temporal(g, b, chunks, first, done=None):
        items = [(s, k) for s in range(2) for k in chunks]
        bias = [temporal_bias(g, s, b) for s in range(2)]

        def score(item):
            s, k = item
            return scores(qall[g, s, pl.ds(k * CROWS, CROWS), :], kbuf[b, s, 0])

        ahead = score(items[0])
        for i, (s, k) in enumerate(items):
            now = ahead
            if i + 1 < len(items):
                ahead = score(items[i + 1])
            rows = pl.ds(k * CROWS, CROWS)
            if first:
                m, acc = jnp.full((CROWS, HD), NEG, F32), None
            else:
                m, acc = m_ref[g, s, rows, :], acc_ref[g, s, rows, :]
            m, acc = fold(now, kbuf[b, s, 1], bias[s], m, acc)
            m_ref[g, s, rows, :] = m
            acc_ref[g, s, rows, :] = acc
            if done is not None and k == CH - 1:
                done(s)

    def o_copies(g, s):
        return (
            remote(osend.at[g, s], orecv.at[4 - g, s], o_ss.at[g, s], o_rs.at[4 - g, s], at_y(g)),
            remote(lsend.at[g, s], lrecv.at[4 - g, s], l_ss.at[g, s], l_rs.at[4 - g, s], at_y(g)),
        )

    def send_o(g, s):
        total = acc_ref[g, s, :, HD:]
        safe = jnp.where(total > 0, total, 1.0)
        osend[g, s] = (acc_ref[g, s, :, :HD] / safe).astype(BF16)
        log = m_ref[g, s] + jnp.log2(safe)
        lsend[g, s] = jnp.transpose(log)[0:8]
        for copy in o_copies(g, s):
            copy.start()

    for s in range(2):
        kc[0][s].wait_recv()
    temporal(0, 0, range(CH), True)
    up[0].wait_recv()
    far = [start(query_copy(3, 2, 0, 1)), None]
    down[1].wait_recv()
    far[1] = start(query_copy(1, 2, 1, 3))
    down[0].wait_recv()
    up[1].wait_recv()
    for g in (1, 3, 2):
        tx[4 - g].wait_recv()
        spread(trecv[g], g)
    h_next = start(remote(wbuf.at[:, :, pl.ds(2 * TILE, TILE)], wbuf.at[:, :, pl.ds(0, TILE)],
                          h_ss.at[0], h_rs.at[0], after))
    h_prev = start(remote(wbuf.at[:, :, pl.ds(TILE, TILE)], wbuf.at[:, :, pl.ds(3 * TILE, TILE)],
                          h_ss.at[1], h_rs.at[1], before))
    temporal(1, 0, range(CH), True)
    temporal(3, 0, range(CH), True)
    for s in range(2):
        kx[s].wait_recv()
        start(kc[1][s])
    load_w.wait()
    mine = pl.ds(pl.multiple_of(c * WROWS, 16), WROWS)
    w_cross = start(remote(w_ref.at[mine, pl.ds(EW, CE)], wx.at[mine], wx_ss.at[0], wx_rs.at[0], x_other))
    w_core = remote(wx.at[mine], wx.at[mine], wx_ss.at[1], wx_rs.at[1], core)
    for copy in far:
        copy.wait_recv()
    temporal(2, 0, range(CH), True)
    for s in range(2):
        kc[1][s].wait_recv()

    @pl.loop(0, 2)
    def _(i):
        g = 1 + 2 * i
        temporal(g, 1, range(CH), False)
        for s in range(2):
            send_o(g, s)

    temporal(2, 1, range(CH), False, lambda s: send_o(2, s))
    temporal(0, 1, range(CH), False)

    h_next.wait_recv()
    h_prev.wait_recv()

    window_bias = [
        rows_bias(lambda half, t=t: window[half][t : t + 1, :]) for t in range(4)
    ]
    items = [(s, k) for s in range(3) for k in range(CH)]
    ahead = scores(qslide[0, 0:CROWS, :], wbuf[0, 0])
    for i, (s, k) in enumerate(items):
        now = ahead
        if i + 1 < len(items):
            s1, k1 = items[i + 1]
            ahead = scores(qslide[s1, k1 * CROWS : (k1 + 1) * CROWS, :], wbuf[s1, 0])
        _, acc = fold(now, wbuf[s, 1], window_bias, jnp.full((CROWS, HD), NEG, F32), None)
        attn[k, :, (s + 2) * HD : (s + 3) * HD] = (acc[:, :HD] / acc[:, HD:]).astype(BF16)

    def combine(k):
        rows = pl.ds(k * CROWS, CROWS)
        for s in range(2):
            total = acc_ref[0, s, rows, HD:]
            logs = [m_ref[0, s, rows, :] + jnp.log2(total)]
            outs = [acc_ref[0, s, rows, :HD] / total]
            for g in range(1, 4):
                line = lrecv[g, s, 0:1, k * CROWS : (k + 1) * CROWS]
                logs.append(jnp.transpose(jnp.broadcast_to(line, (HD, CROWS))))
                outs.append(orecv[g, s, rows, :].astype(F32))
            top = functools.reduce(jnp.maximum, logs)
            weights = [jnp.exp2(log - top) for log in logs]
            mixed = functools.reduce(jnp.add, [w * o for w, o in zip(weights, outs)])
            attn[k, :, s * HD : (s + 1) * HD] = (
                mixed / functools.reduce(jnp.add, weights)
            ).astype(BF16)

    WIDTH = 768

    def reorder(k):
        slots = [attn[k, :, s * HD : (s + 1) * HD] for s in range(5)]
        for i in range(5):
            value = slots[0]
            for s in range(1, 5):
                if i in heads_of[s]:
                    value = lax.select(order[s] == i, slots[s], value)
            attn[k, :, i * HD : (i + 1) * HD] = value

    def project(k, first, last):
        whole = (last - first) // WIDTH

        @pl.loop(0, whole)
        def _(j):
            columns = pl.ds(pl.multiple_of(first + j * WIDTH, 128), WIDTH)
            pbuf[k, :, columns] = dot(attn[k], w_ref[:, columns], 1, 0).astype(BF16)

        rest = first + whole * WIDTH
        if rest < last:
            pbuf[k, :, rest:last] = dot(attn[k], w_ref[:, rest:last], 1, 0).astype(BF16)

    def exchange(k):
        for zr in range(4):
            at = (zr * 2 + 1) * DROWS
            asend[k, zr * DROWS : (zr + 1) * DROWS, :] = attn[k, at : at + DROWS, :]
        return start(remote(asend.at[k], arecv.at[k], a_ss.at[k], a_rs.at[k], x_other))

    def project_two(k):
        kept = jnp.concatenate(
            [attn[k, zr * ZROWS : zr * ZROWS + DROWS, :] for zr in range(4)], axis=0
        )

        @pl.loop(0, CE // 512)
        def _(j):
            columns = pl.ds(pl.multiple_of(EW + j * 512, 512), 512)
            others = pl.ds(pl.multiple_of(j * 512, 512), 512)
            value = dot(kept, w_ref[:, columns], 1, 0) + dot(arecv[k], wx[:, others], 1, 0)
            value = value.astype(BF16)
            for zr in range(4):
                pbuf[k, zr * ZROWS : zr * ZROWS + DROWS, columns] = value[zr * DROWS : (zr + 1) * DROWS]

    def block(k, zr, xr, first, width):
        return pbuf.at[k, pl.ds((zr * 2 + xr) * DROWS, DROWS), pl.ds(first, width)]

    def add(k, zr, xr, first, width, *others):
        @pl.loop(0, DROWS // 16)
        def _(i):
            rows = pl.ds(pl.multiple_of((zr * 2 + xr) * DROWS + i * 16, 16), 16)
            value = pbuf[k, rows, first : first + width].astype(F32)
            for other in others:
                value += other[pl.ds(pl.multiple_of(i * 16, 16), 16), :].astype(F32)
            pbuf[k, rows, first : first + width] = value.astype(BF16)

    def emit(k, first, width, *others):
        @pl.loop(0, DROWS // 16)
        def _(i):
            value = pbuf[k, pl.ds(pl.multiple_of(i * 16, 16), 16), first : first + width].astype(F32)
            for other in others:
                value += other[pl.ds(pl.multiple_of(i * 16, 16), 16), :].astype(F32)
            rows = pl.ds(pl.multiple_of(k * DROWS + i * 16, 16), 16)
            out_ref[rows, first : first + width] = value.astype(BF16)

    H1, H2 = CA, CA + HB

    class Chunk:
        def __init__(self, k):
            self.k = k
            self.count = 0

        def send(self, src, dst, peer):
            n = self.count
            self.count += 1
            return start(remote(src, dst, r_ss.at[self.k, n], r_rs.at[self.k, n], peer))

        def first_a(self):
            k = self.k
            self.fa = [
                self.send(block(k, 2, 0, 0, CA), fa.at[k, 0], z_up),
                self.send(block(k, 2, 1, 0, CA), fa.at[k, 1], z_down),
            ]
            self.ra = [
                self.send(block(k, 1, 1, 0, CA), ra.at[k, 0, 1], z_up),
                self.send(block(k, 3, 0, 0, CA), ra.at[k, 1, 0], z_down),
            ]

        def first_b(self):
            k = self.k
            self.xb = {}
            for zr in (2, 1, 3, 0):
                self.xb[zr] = self.send(block(k, zr, 1, CA, CB), xb.at[k, zr], x_other)

        def forward_a(self):
            k = self.k
            self.fa[0].wait_recv()
            add(k, 1, 0, 0, CA, fa.at[k, 0])
            self.ra.append(self.send(block(k, 1, 0, 0, CA), ra.at[k, 0, 0], z_up))
            self.fa[1].wait_recv()
            add(k, 3, 1, 0, CA, fa.at[k, 1])
            self.ra.append(self.send(block(k, 3, 1, 0, CA), ra.at[k, 1, 1], z_down))

        def second_b(self):
            k = self.k
            self.xb[2].wait_recv()
            add(k, 2, 0, CA, CB, xb.at[k, 2])
            self.fb = [
                self.send(block(k, 2, 0, H1, HB), fb.at[k, 0], z_up),
                self.send(block(k, 2, 0, H2, HB), fb.at[k, 1], z_down),
            ]
            self.xb[1].wait_recv()
            add(k, 1, 0, CA, CB, xb.at[k, 1])
            self.rb = [self.send(block(k, 1, 0, H2, HB), rb.at[k, 0, 1], z_up)]
            self.xb[3].wait_recv()
            add(k, 3, 0, CA, CB, xb.at[k, 3])
            self.rb.append(self.send(block(k, 3, 0, H1, HB), rb.at[k, 1, 0], z_down))

        def first_e(self):
            k = self.k
            self.fe = [
                self.send(block(k, 2, 0, EW, HE), fe.at[k, 0], z_up),
                self.send(block(k, 2, 0, EW + HE, HE), fe.at[k, 1], z_down),
            ]
            self.re = [
                self.send(block(k, 1, 0, EW + HE, HE), re.at[k, 0, 1], z_up),
                self.send(block(k, 3, 0, EW, HE), re.at[k, 1, 0], z_down),
            ]

        def forward_e(self):
            k = self.k
            self.fe[0].wait_recv()
            add(k, 1, 0, EW, HE, fe.at[k, 0])
            self.re.append(self.send(block(k, 1, 0, EW, HE), re.at[k, 0, 0], z_up))
            self.fe[1].wait_recv()
            add(k, 3, 0, EW + HE, HE, fe.at[k, 1])
            self.re.append(self.send(block(k, 3, 0, EW + HE, HE), re.at[k, 1, 1], z_down))

        def finish_e(self):
            k = self.k
            for copy in self.re:
                copy.wait_recv()
            emit(k, EW, HE, re.at[k, 0, 0], re.at[k, 1, 0])
            emit(k, EW + HE, HE, re.at[k, 0, 1], re.at[k, 1, 1])

        def third_a(self):
            k = self.k
            for copy in self.ra:
                copy.wait_recv()
            add(k, 0, 1, 0, CA, ra.at[k, 0, 1], ra.at[k, 1, 1])
            self.xa = self.send(block(k, 0, 1, 0, CA), xa.at[k], x_other)

        def forward_b(self):
            k = self.k
            self.fb[0].wait_recv()
            add(k, 1, 0, H1, HB, fb.at[k, 0])
            self.rb.append(self.send(block(k, 1, 0, H1, HB), rb.at[k, 0, 0], z_up))
            self.fb[1].wait_recv()
            add(k, 3, 0, H2, HB, fb.at[k, 1])
            self.rb.append(self.send(block(k, 3, 0, H2, HB), rb.at[k, 1, 1], z_down))

        def finish(self):
            k = self.k
            self.xa.wait_recv()
            emit(k, 0, CA, ra.at[k, 0, 0], ra.at[k, 1, 0], xa.at[k])
            self.xb[0].wait_recv()
            for copy in self.rb:
                copy.wait_recv()
            emit(k, H1, HB, xb.at[k, 0, :, pl.ds(0, HB)], rb.at[k, 0, 0], rb.at[k, 1, 0])
            emit(k, H2, HB, xb.at[k, 0, :, pl.ds(HB, HB)], rb.at[k, 0, 1], rb.at[k, 1, 1])

    one, two = Chunk(0), Chunk(1)
    for g in (1, 3, 2):
        for s in range(2):
            for copy in o_copies(4 - g, s):
                copy.wait_recv()
    combine(0)
    reorder(0)
    crossed = [exchange(0)]
    project(0, CA, EW)
    one.first_b()
    project(0, 0, CA)
    one.first_a()
    w_cross.wait_recv()
    start(w_core)
    combine(1)
    reorder(1)
    crossed.append(exchange(1))
    one.forward_a()
    project(1, CA, EW)
    two.first_b()
    project(1, 0, CA)
    two.first_a()
    w_core.wait_recv()
    crossed[0].wait_recv()
    project_two(0)
    one.first_e()
    two.forward_a()
    crossed[1].wait_recv()
    project_two(1)
    two.first_e()
    one.forward_e()
    one.second_b()
    one.third_a()
    two.forward_e()
    one.forward_b()
    two.second_b()
    two.third_a()
    two.forward_b()
    one.finish_e()
    two.finish_e()
    one.finish()
    two.finish()

    for copy in sent:
        copy.wait_send()
    for g in range(1, 4):
        for s in range(2):
            for copy in o_copies(g, s):
                copy.wait_send()


def per_device(queries, keys_values, head_kind, tile_neighbours, tile_mask, out_weight):
    smem = pl.BlockSpec(memory_space=pltpu.SMEM)
    vmem = pl.BlockSpec(memory_space=pltpu.VMEM)
    dma = pltpu.SemaphoreType.DMA
    return pl.pallas_call(
        kernel,
        out_shape=jax.ShapeDtypeStruct((ROWS // 8, D), BF16),
        in_specs=[
            smem, smem, smem,
            vmem, vmem,
            pl.BlockSpec(memory_space=pl.ANY),
        ],
        out_specs=vmem,
        scratch_shapes=[
            pltpu.VMEM((5 * HD, D), BF16),
            pltpu.VMEM((4, 2, ROWS, HD), BF16),
            pltpu.VMEM((3, ROWS, HD), BF16),
            pltpu.VMEM((2, 2, 2, 2 * ROWS, HD), BF16),
            pltpu.VMEM((3, 2, 4 * TILE, HD), BF16),
            pltpu.VMEM((8, HD), F32),
            pltpu.VMEM((4, 8, HD), F32),
            pltpu.VMEM((4, 4, 32, HD), F32),
            pltpu.VMEM((4, 2, ROWS, HD), F32),
            pltpu.VMEM((4, 2, ROWS, 2 * HD), F32),
            pltpu.VMEM((4, 2, ROWS, HD), BF16),
            pltpu.VMEM((4, 2, 8, ROWS), F32),
            pltpu.VMEM((4, 2, ROWS, HD), BF16),
            pltpu.VMEM((4, 2, 8, ROWS), F32),
            pltpu.VMEM((CH, CROWS, 5 * HD), BF16),
            pltpu.VMEM((CH, CROWS, D), BF16),
            pltpu.VMEM((CH, 2, DROWS, CA), BF16),
            pltpu.VMEM((CH, 2, 2, DROWS, CA), BF16),
            pltpu.VMEM((CH, DROWS, CA), BF16),
            pltpu.VMEM((CH, 4, DROWS, CB), BF16),
            pltpu.VMEM((CH, 2, DROWS, HB), BF16),
            pltpu.VMEM((CH, 2, 2, DROWS, HB), BF16),
            pltpu.VMEM((5 * HD, CE), BF16),
            pltpu.VMEM((CH, CROWS // 2, 5 * HD), BF16),
            pltpu.VMEM((CH, CROWS // 2, 5 * HD), BF16),
            pltpu.VMEM((CH, 2, DROWS, HE), BF16),
            pltpu.VMEM((CH, 2, 2, DROWS, HE), BF16),
            dma,
            dma((4, 2)), dma((4, 2)),
            dma((4,)), dma((4,)),
            dma((2,)), dma((2,)),
            dma((2, 2)), dma((2, 2)),
            dma((2,)), dma((2,)),
            dma((4, 2)), dma((4, 2)),
            dma((4, 2)), dma((4, 2)),
            dma((CH, 30)), dma((CH, 30)),
            dma((2,)), dma((2,)),
            dma((CH,)), dma((CH,)),
        ],
        name="attend_project",
        compiler_params=pltpu.CompilerParams(
            collective_id=0, has_side_effects=True, vmem_limit_bytes=60 * 2**20
        ),
    )(
        head_kind,
        tile_neighbours,
        tile_mask,
        jnp.transpose(queries, (1, 0, 2)),
        jnp.transpose(keys_values, (0, 2, 1, 3)),
        out_weight,
    )


def solution(mesh):
    return jax.shard_map(
        per_device,
        mesh=mesh,
        in_specs=(
            P("frame", "head", None),
            P(None, "frame", "head", None),
            P("head"),
            P("frame", None),
            P("frame", None),
            P("head", None),
        ),
        out_specs=P(("frame", "head"), None),
        check_vma=False,
    )
```
